256 devices in a mesh: sub: 64 (over z, y, core), front: 4 (over x).
Axes of the slice: x: 4, y: 4, z: 8, core: 2. Of those that a mesh axis runs over, the one named last changes fastest.
Arguments:
- panels: bfloat16 [64, 3072, 3072], P('sub', 'front'), as said below
- gap: float32 [64, 4, 8, 768], P('sub', 'front'), as said below
- modes: float32 [64, 4, 6, 768], P('sub', 'front'), as said below
- mode_loads: float32 [64, 6, 8], P('sub'), may hold values from -6 to 6
- partners: int32 [64, 4], P('sub', 'front'), may hold values from -1 to 63, as said below
- counts: int32 [64], replicated, may hold values from 0 to 6, as said below
Outputs:
- multipliers: float32 [64, 4, 8, 768], P('sub', 'front')
- projected: float32 [64, 4, 8, 768], P('sub', 'front')
The draws below stay inside these ranges and needn't reach their ends.
Inputs may be any that keep to these rules, and one draw needn't show every extreme that they name: If partners[s, j] = p >= 0 then p != s and partners[p, j] = s; slots 0 and 1 of every subdomain are used, and the graph of subdomains joined by used slots is connected. `counts`: some subdomain has 0 rigid-body modes, so coarse is positive definite. `panels`: each subdomain's matrix is symmetric and positive definite. `gap`: the two sides of a joint hold equal values. `modes`: the two sides of a joint hold equal values.
All inputs are finite; a program needn't handle non-finite values.
Results may differ from the reference program's by a relative error of at most 0.0092.
The reference program's roundings to bfloat16 on the way count: a program that leaves them out, or rounds other values in their place, can miss the bound.
Values may be sent and summed in bfloat16 or wider, within the bound.
No kernel may reach another device: no remote copies, remote signals or barrier semaphores. Data moves between devices by JAX's collectives and lax.ppermute only.
A program may use at most 64 MiB of HBM per device.

```python
import math
import jax
import jax.numpy as jnp
from jax import lax

M = 768
MODES = 6
ITERS = 2
NRHS = 8
JOINTS = 4
NB = 3072
NC = 384
N_SUB = 64


def joint_layout(key):
    base = jax.random.fold_in(key, 11)
    halves = N_SUB // 2
    partner_cols = []
    mate_cols = []
    pair_cols = []
    used_cols = []
    cycle_order = jax.random.permutation(jax.random.fold_in(base, 0), N_SUB)
    cycle_position = jnp.argsort(cycle_order)
    for slot in range(JOINTS):
        if slot == 0:
            position = cycle_position
            other = cycle_order[position + 1 - 2 * (position % 2)]
            pair = position // 2
            keep = jnp.ones((halves,), jnp.bool_)
        elif slot == 1:
            position = cycle_position
            odd = position % 2
            other = jnp.where(odd == 1, cycle_order[(position + 1) % N_SUB], cycle_order[(position - 1) % N_SUB])
            pair = jnp.where(odd == 1, (position - 1) // 2, (position // 2 - 1) % halves)
            keep = jnp.ones((halves,), jnp.bool_)
        else:
            order = jax.random.permutation(jax.random.fold_in(base, slot), N_SUB)
            position = jnp.argsort(order)
            other = order[position + 1 - 2 * (position % 2)]
            pair = position // 2
            votes = jax.random.randint(jax.random.fold_in(base, 100 + slot), (halves,), 0, 4)
            keep = votes > 0
            if slot == JOINTS - 1:
                keep = keep & (jnp.arange(halves) > 0)
        kept = keep[pair]
        partner_cols.append(jnp.where(kept, other, -1).astype(jnp.int32))
        mate_cols.append(other.astype(jnp.int32))
        pair_cols.append(pair.astype(jnp.int32))
        used_cols.append(kept.astype(jnp.float32))
    return (jnp.stack(partner_cols, 1), jnp.stack(mate_cols, 1), jnp.stack(pair_cols, 1), jnp.stack(used_cols, 1))


def draw_partners(key, part):
    return joint_layout(key)[0]


def draw_counts(key, part):
    values = jax.random.randint(jax.random.fold_in(key, 61), (N_SUB,), 0, MODES + 1)
    zero_at = jax.random.randint(jax.random.fold_in(key, 62), (), 0, N_SUB)
    full_at = (zero_at + 1 + jax.random.randint(jax.random.fold_in(key, 63), (), 0, N_SUB - 1)) % N_SUB
    places = jnp.arange(N_SUB)
    values = jnp.where(places == zero_at, 0, values)
    values = jnp.where(places == full_at, MODES, values)
    return values.astype(jnp.int32)


def draw_gap(key, part):
    partner_ids, mates, pairs, used = joint_layout(key)
    shape = (JOINTS, N_SUB // 2, NRHS, M)
    raw = jax.random.normal(jax.random.fold_in(key, 21), shape)
    picked = raw[jnp.arange(JOINTS)[None, :], pairs]
    lower = jnp.minimum(jnp.arange(N_SUB)[:, None], mates).astype(jnp.float32)
    scale = 2.0 * (1.0 + 2.0 * lower / (N_SUB - 1))
    return (picked * scale[:, :, None, None] * used[:, :, None, None]).astype(jnp.float32)


def draw_modes(key, part):
    partner_ids, mates, pairs, used = joint_layout(key)
    shape = (JOINTS, N_SUB // 2, MODES, M)
    raw = jax.random.normal(jax.random.fold_in(key, 41), shape)
    picked = raw[jnp.arange(JOINTS)[None, :], pairs]
    return (picked * (1.0 / math.sqrt(M))).astype(jnp.float32)


def draw_panels(key, part):
    keys = jax.random.split(jax.random.fold_in(key, 31), N_SUB)
    identity = jnp.eye(NB, dtype=jnp.float32)

    def one_panel(sub_key):
        noise = jnp.clip(jax.random.normal(jax.random.fold_in(sub_key, 1), (NB, NB)), -4.0, 4.0)
        sym = (noise + noise.T) * (0.65 / math.sqrt(NB))
        diagonal = jax.random.uniform(jax.random.fold_in(sub_key, 2), (NB,), minval=2.4, maxval=4.4)
        matrix = sym * (1.0 - identity) + identity * diagonal[None, :]
        return matrix.astype(jnp.bfloat16)
    return lax.map(one_panel, keys)


def steps_of(key, extent, shards, least, top_value):
    gain = 1.0
    for dim, blocks in shards:
        heights = jax.random.uniform(jax.random.fold_in(jax.random.fold_in(key, 6), dim), (blocks,), jnp.float32, least / len(shards), top_value / len(shards))
        gain = gain * jnp.repeat(jnp.exp(heights), extent[dim] // blocks).reshape((-1,) + (1,) * (len(extent) - 1 - dim))
    return gain


def gaussian(rng, dims, deviation, bound, pieces=(), held_as=jnp.bfloat16):
    array = deviation * jax.random.normal(rng, dims, jnp.float32)
    if pieces:
        array = array * steps_of(rng, dims, pieces, -0.22, 0.18)
    return jnp.clip(array, -bound, bound).astype(held_as)


def setup_inputs(seed: int = 0) -> dict:
    key_list = jax.random.split(jax.random.key(seed), 7)
    panels = draw_panels(jax.random.fold_in(key_list[6], 71), 0)
    gap = draw_gap(jax.random.fold_in(key_list[6], 71), 0)
    modes = draw_modes(jax.random.fold_in(key_list[6], 71), 0)
    mode_loads = gaussian(key_list[3], (N_SUB, MODES, NRHS), 1.0, 6.0, ((0, 64),), jnp.float32)
    partners = draw_partners(jax.random.fold_in(key_list[6], 71), 0)
    counts = draw_counts(jax.random.fold_in(key_list[6], 71), 0)
    return dict(panels=panels, gap=gap, modes=modes, mode_loads=mode_loads, partners=partners, counts=counts)


def reference(panels, gap, modes, mode_loads, partners, counts):
    highest = lax.Precision.HIGHEST
    used = (partners >= 0).astype(jnp.float32)
    mate = jnp.maximum(partners, 0)
    own = jnp.arange(N_SUB, dtype=jnp.int32)[:, None]
    side = jnp.where(own < partners, 1.0, -1.0).astype(jnp.float32)
    active = (jnp.arange(MODES, dtype=jnp.int32)[None, :] < counts[:, None]).astype(jnp.float32)
    gram = jnp.einsum('sjkm,sjlm->sjkl', modes, modes, precision=highest) * used[:, :, None, None]
    identity = jnp.eye(N_SUB, dtype=jnp.float32)
    mates = (mate[:, :, None] == jnp.arange(N_SUB, dtype=jnp.int32)[None, None, :]).astype(jnp.float32) * used[:, :, None]
    placed = identity[:, None, :] - mates
    coarse = jnp.einsum('sjkl,sjt,sk,tl->sktl', gram, placed, active, active, precision=highest)
    coarse = coarse.reshape(NC, NC) + jnp.diag(1.0 - active.reshape(-1))
    factor = jnp.linalg.cholesky(coarse)
    weight = side * used

    def coarse_solve(rhs):
        return jax.scipy.linalg.cho_solve((factor, True), rhs)

    def expand(values):
        shaped = values.reshape(N_SUB, MODES, NRHS) * active[:, :, None]
        theirs = shaped[mate]
        coeff = side[:, :, None, None] * (shaped[:, None] - theirs)
        return used[:, :, None, None] * jnp.einsum('sjkn,sjkm->sjnm', coeff, modes, precision=highest)

    def mode_terms(resid):
        sums = jnp.einsum('sjkm,sjnm->skn', modes * weight[:, :, None, None], resid, precision=highest)
        return (sums * active[:, :, None]).reshape(NC, NRHS)

    def dual(vector):
        loads = (weight[:, :, None, None] * vector).astype(jnp.bfloat16)
        loads = loads.transpose(0, 2, 1, 3).reshape(N_SUB, NRHS, NB)

        def one_sub(pair):
            return lax.dot_general(pair[0].astype(jnp.float32), pair[1].astype(jnp.float32), (((1,), (1,)), ((), ())), preferred_element_type=jnp.float32)
        moved = lax.map(one_sub, (loads, panels))
        moved = moved.reshape(N_SUB, NRHS, JOINTS, M).transpose(0, 2, 1, 3)
        theirs = moved[mate, jnp.arange(JOINTS, dtype=jnp.int32)[None, :]]
        return weight[:, :, None, None] * (moved - theirs)

    def weighted_dot(first, second):
        return 0.5 * jnp.sum(first * second, axis=(0, 1, 3))

    def project(resid):
        return resid - expand(coarse_solve(mode_terms(resid)))
    start_loads = (mode_loads * active[:, :, None]).reshape(NC, NRHS)
    multipliers = expand(coarse_solve(start_loads))
    residual = used[:, :, None, None] * gap - dual(multipliers)
    projected = project(residual)
    rho = weighted_dot(projected, projected)
    direction = projected
    for step in range(ITERS):
        image = dual(direction)
        alpha = rho / weighted_dot(direction, image)
        multipliers = multipliers + alpha[None, None, :, None] * direction
        residual = residual - alpha[None, None, :, None] * image
        projected = project(residual)
        rho_new = weighted_dot(projected, projected)
        direction = projected + (rho_new / rho)[None, None, :, None] * direction
        rho = rho_new
    return (multipliers, projected)
```

```python
import functools

import jax
import jax.numpy as jnp
from jax import lax
from jax.experimental import pallas as pl
from jax.experimental.pallas import tpu as pltpu
from jax.sharding import Mesh, PartitionSpec as P

MODES = 6
NRHS = 8
M = 768
SUBS = 64
PAD = 8
NP = SUBS * PAD
BLK = 128
HALF = SUBS // 2
HIGHEST = lax.Precision.HIGHEST
F32 = jnp.float32
BF16 = jnp.bfloat16

LANE_DU, LANE_ZZ, LANE_FF = 8, 9, 10
W_U = M + 128
W_X = M + NP + 128

SMEM = pl.BlockSpec(memory_space=pltpu.SMEM)
VMEM = pl.BlockSpec(memory_space=pltpu.VMEM)
ANY = pl.BlockSpec(memory_space=pl.ANY)
PARAMS = pltpu.CompilerParams(vmem_limit_bytes=40 * 1024 * 1024)


def lanes(shape):
    return lax.broadcasted_iota(jnp.int32, shape, len(shape) - 1)


def rows_of(shape):
    return lax.broadcasted_iota(jnp.int32, shape, 0)


def dot_high(a, b):
    return jnp.dot(a, b, precision=HIGHEST, preferred_element_type=F32)


def coarse_kernel(cnt_ref, me_ref, own_ref, oth_ref, inv_ref, y0_ref, yg_ref, g_ref, a_ref, d_ref):
    g_ref[0:NP // 2, :] = own_ref[...]
    g_ref[NP // 2:NP, :] = oth_ref[...]
    core, y_me = me_ref[0], me_ref[1]
    row_1 = rows_of((BLK, 1))
    col_1 = lanes((1, NP))
    col_sub = lax.shift_right_logical(col_1, 3)
    col_mode = lax.bitwise_and(col_1, 7)
    spread = (rows_of((PAD, NP)) == lax.bitwise_and(lanes((PAD, NP)), 7)).astype(F32)
    flipped = g_ref[...].T
    col_count = flipped[7:8, :].astype(jnp.int32)
    col_active = (col_mode < col_count).astype(F32)
    for b in range(NP // BLK):
        rows = g_ref[b * BLK:(b + 1) * BLK, :]
        row_id = row_1 + b * BLK
        row_sub = lax.shift_right_logical(row_id, 3)
        row_active = (lax.bitwise_and(row_id, 7) < rows[:, 7:8].astype(jnp.int32)).astype(F32)
        total = jnp.zeros((BLK, NP), F32)
        same = (row_sub == col_sub).astype(F32)
        for k in range(4):
            mate = rows[:, 8 * k + 6:8 * k + 7].astype(jnp.int32)
            used = (mate >= 0).astype(F32)
            place = (
                lax.bitwise_xor(lax.bitwise_and(mate, 1), core) * HALF
                + lax.bitwise_and(y_me - lax.shift_right_logical(mate, 1), 3) * 8
                + lax.shift_right_logical(mate, 3)
            )
            gram = jnp.where(lanes((BLK, PAD)) < MODES, rows[:, 8 * k:8 * k + 8], 0.0)
            wide = dot_high(gram * (used * row_active), spread)
            total = total + wide * (same - (place == col_sub).astype(F32))
        total = total * col_active
        total = total + jnp.where(row_id == col_1, 1.0 - row_active, 0.0)
        a_ref[b * BLK:(b + 1) * BLK, :] = total

    lane = lanes((BLK, BLK))
    lane_1 = lanes((1, BLK))

    def sweep_pair(p):
        mat = d_ref[...]
        r0, r1 = mat[p:p + 1, :], mat[p + 1:p + 2, :]
        c0, c1 = mat[:, p:p + 1], mat[:, p + 1:p + 2]
        top, off, low = r0[:, p:p + 1], r0[:, p + 1:p + 2], r1[:, p + 1:p + 2]
        over = 1.0 / top
        ratio = off * over
        g = 1.0 / (low - off * ratio)
        f = -ratio * g
        e = over + ratio * ratio * g
        n0 = e * r0 + f * r1
        n1 = f * r0 + g * r1
        new = mat - c0 * n0 - c1 * n1
        new = jnp.where(lane == p, c0 * e + c1 * f, new)
        new = jnp.where(lane == p + 1, c0 * f + c1 * g, new)
        d_ref[...] = new
        d_ref[p:p + 1, :] = jnp.where(lane_1 == p, -e, jnp.where(lane_1 == p + 1, -f, n0))
        d_ref[p + 1:p + 2, :] = jnp.where(lane_1 == p, -f, jnp.where(lane_1 == p + 1, -g, n1))

    for b in range(NP // BLK):
        lo, hi = b * BLK, (b + 1) * BLK
        d_ref[...] = a_ref[lo:hi, lo:hi]

        for i in range(BLK // PAD):
            for h in range(MODES // 2):
                @pl.when(cnt_ref[b * (BLK // PAD) + i] > 2 * h)
                def _(p=PAD * i + 2 * h):
                    sweep_pair(p)

        small = -d_ref[...]
        tall = a_ref[:, lo:hi]
        wide = dot_high(small, a_ref[lo:hi, :])
        a_ref[...] = a_ref[...] - dot_high(tall, wide)
        a_ref[:, lo:hi] = dot_high(tall, small)
        a_ref[lo:hi, :] = wide
        a_ref[lo:hi, lo:hi] = -small
    inverse = -a_ref[...]
    inv_ref[...] = inverse
    y = dot_high(flipped[32:48, :], inverse)
    for b in range(NP // BLK):
        y0_ref[b] = y[0:8, b * BLK:(b + 1) * BLK]
        yg_ref[b] = y[8:16, b * BLK:(b + 1) * BLK]


def mate_kernel(with_norm, mate_ref, cnt_ref, me_ref, w_ref, own_ref, oth_ref, out_ref, g_ref, sems):
    first = pltpu.make_async_copy(own_ref, g_ref.at[0:HALF], sems.at[0])
    second = pltpu.make_async_copy(oth_ref, g_ref.at[HALF:SUBS], sems.at[1])
    first.start()
    second.start()
    first.wait()
    second.wait()
    mine = me_ref[2]
    theirs = jnp.maximum(mate_ref[mine], 0)
    out_ref[:, 0:M] = w_ref[0] * (g_ref[mine][:, 0:M] - g_ref[theirs][:, 0:M])
    lane = lanes((NRHS, 128))
    sums = [jnp.zeros((NRHS, 128), F32) for _ in range(NP // BLK)]
    scalars = jnp.zeros((NRHS, 128), F32)
    norm = jnp.zeros((NRHS, M), F32)
    for p in range(SUBS):
        mate = mate_ref[p]
        used = (mate >= 0).astype(F32)
        at = jnp.maximum(mate, 0)
        tile = g_ref[p, :, M:W_U]
        scalars = scalars + tile
        limit = jnp.where(mate >= 0, cnt_ref[p], 0)
        piece = jnp.where(lane < limit, tile - g_ref[at, :, M:W_U], 0.0)
        if p % 16:
            piece = pltpu.roll(piece, 8 * (p % 16), 1)
        sums[p // 16] = sums[p // 16] + piece
        if with_norm:
            gone = g_ref[p, :, 0:M] - g_ref[at, :, 0:M]
            norm = norm + used * (gone * gone)
    for b in range(NP // BLK):
        out_ref[:, M + b * BLK:M + (b + 1) * BLK] = sums[b]
    if with_norm:
        scalars = jnp.where(lane == LANE_FF, 0.5 * jnp.sum(norm, axis=1, keepdims=True), scalars)
    out_ref[:, M + NP:W_X] = scalars


def y_at(y_ref, place):
    tile = y_ref[lax.div(place, 16)]
    return pltpu.roll(tile, lax.rem(128 - 8 * lax.rem(place, 16), 128), 1)


def expand(y_ref, me_ref, w_ref, modes_ref, k):
    coeff = y_at(y_ref, me_ref[2]) - y_at(y_ref, me_ref[4 + k])
    total = coeff[:, 0:1] * modes_ref[k, 0:1, :]
    for m in range(1, MODES):
        total = total + coeff[:, m:m + 1] * modes_ref[k, m:m + 1, :]
    return w_ref[k] * total


def start_panel(me_ref, panel_ref, pan_ref, sems):
    copies = []
    for k in range(4):
        at = pl.multiple_of(lax.bitwise_and(me_ref[3] - k, 3) * M, M)
        copy = pltpu.make_async_copy(panel_ref.at[0, :, pl.ds(at, M)], pan_ref.at[k], sems.at[k])
        copy.start()
        copies.append(copy)
    return copies


def apply_panel(copies, w_ref, modes_ref, vectors, pan_ref, pay_ref, square):
    total = None
    for k in range(4):
        load = (w_ref[k] * vectors[k]).astype(BF16)
        copies[k].wait()
        part = lax.dot_general(load, pan_ref[k], (((1,), (1,)), ((), ())), preferred_element_type=F32)
        total = part if total is None else total + part
    lane = lanes((NRHS, 128))
    tail = jnp.zeros((NRHS, 128), F32)
    for m in range(MODES):
        tail = jnp.where(lane == m, jnp.sum(total * modes_ref[0, m:m + 1, :], axis=1, keepdims=True), tail)
    dots = jnp.sum(w_ref[0] * vectors[0] * total, axis=1, keepdims=True)
    tail = jnp.where(lane == LANE_DU, dots, tail)
    if square is not None:
        tail = jnp.where(lane == LANE_ZZ, 0.5 * jnp.sum(square * square, axis=1, keepdims=True), tail)
    pay_ref[:, 0:M] = total
    pay_ref[:, M:W_U] = tail


def begin_kernel(me_ref, w_ref, y_ref, modes_ref, panel_ref, lam_ref, pay_ref, pan_ref, sems):
    copies = start_panel(me_ref, panel_ref, pan_ref, sems)
    vectors = [expand(y_ref, me_ref, w_ref, modes_ref, k) for k in range(4)]
    lam_ref[...] = vectors[0]
    apply_panel(copies, w_ref, modes_ref, vectors, pan_ref, pay_ref, None)


def gathered_sums(x_refs, inv_ref):
    ms = x_refs[0][:, M:M + NP]
    scalars = x_refs[0][:, M + NP:W_X]
    for ref in x_refs[1:]:
        ms = ms + ref[:, M:M + NP]
        scalars = scalars + ref[:, M + NP:W_X]
    return ms, dot_high(ms, inv_ref[...]), scalars


def first_kernel(me_ref, w_ref, x0, x1, x2, x3, inv_ref, yg_ref, gap_ref, modes_ref, panel_ref,
                 r_ref, z_ref, y_ref, pay_ref, pan_ref, sems):
    copies = start_panel(me_ref, panel_ref, pan_ref, sems)
    xs = (x0, x1, x2, x3)
    _, solved, _ = gathered_sums(xs, inv_ref)
    for b in range(NP // BLK):
        y_ref[b] = yg_ref[b] - solved[:, b * BLK:(b + 1) * BLK]
    vectors = []
    for k in range(4):
        resid = w_ref[k] * w_ref[k] * gap_ref[k] - xs[k][:, 0:M]
        r_ref[k] = resid
        z = resid - expand(y_ref, me_ref, w_ref, modes_ref, k)
        z_ref[k] = z
        vectors.append(z)
    apply_panel(copies, w_ref, modes_ref, vectors, pan_ref, pay_ref, vectors[0])


def second_kernel(me_ref, w_ref, x0, x1, x2, x3, inv_ref, y_ref, r_ref, d_ref, lam_ref, modes_ref, panel_ref,
                  r_out, d_out, y_out, lam_out, rho_out, pay_ref, pan_ref, sems):
    copies = start_panel(me_ref, panel_ref, pan_ref, sems)
    xs = (x0, x1, x2, x3)
    ms, solved, scalars = gathered_sums(xs, inv_ref)
    rho = scalars[:, LANE_ZZ:LANE_ZZ + 1]
    alpha = rho / scalars[:, LANE_DU:LANE_DU + 1]
    squared = scalars[:, LANE_FF:LANE_FF + 1] - jnp.sum(ms * solved, axis=1, keepdims=True)
    rho_new = jnp.maximum(alpha * alpha * squared - rho, 0.0)
    beta = rho_new / rho
    for b in range(NP // BLK):
        y_out[b] = y_ref[b] - alpha * solved[:, b * BLK:(b + 1) * BLK]
    vectors = []
    for k in range(4):
        resid = r_ref[k] - alpha * xs[k][:, 0:M]
        direction = resid - expand(y_out, me_ref, w_ref, modes_ref, k) + beta * d_ref[k]
        vectors.append(direction)
        if k == 0:
            r_out[...] = resid
            d_out[...] = direction
    lam_out[...] = lam_ref[...] + alpha * d_ref[0]
    rho_out[...] = jnp.broadcast_to(rho_new, (NRHS, 128))
    apply_panel(copies, w_ref, modes_ref, vectors, pan_ref, pay_ref, None)


def last_kernel(me_ref, w_ref, x0, x1, x2, x3, inv_ref, y_ref, r_ref, d_ref, lam_ref, rho_ref, modes_ref,
                lam_out, z_out, y_out):
    xs = (x0, x1, x2, x3)
    _, solved, scalars = gathered_sums(xs, inv_ref)
    alpha = rho_ref[:, 0:1] / scalars[:, LANE_DU:LANE_DU + 1]
    for b in range(NP // BLK):
        y_out[b] = y_ref[b] - alpha * solved[:, b * BLK:(b + 1) * BLK]
    resid = r_ref[...] - alpha * x0[:, 0:M]
    lam_out[...] = lam_ref[...] + alpha * d_ref[...]
    z_out[...] = resid - expand(y_out, me_ref, w_ref, modes_ref, 0)


def shift(value, axis, step):
    size = lax.axis_size(axis)
    return lax.ppermute(value, axis, [(i, (i + step) % size) for i in range(size)])


def front_gather(value):
    return [value] + [shift(value, "x", k) for k in range(1, 4)]


def sub_gather(value):
    width = value.shape[-1]
    copies = jnp.broadcast_to(value[None], (8,) + value.shape)
    along_z = lax.all_to_all(copies, "z", 0, 0, tiled=True)
    own = jnp.concatenate([along_z] + [shift(along_z, "y", k) for k in range(1, 4)], axis=0)
    other = shift(own, "c", 1)
    return own.reshape(HALF, NRHS, width), other.reshape(HALF, NRHS, width)


def sds(*shape):
    return jax.ShapeDtypeStruct(shape, F32)


def shards(panels, gap, modes, mode_loads, partners, counts):
    z_me, y_me, c_me, x_me = (lax.axis_index(a) for a in ("z", "y", "c", "x"))
    own = (z_me * 4 + y_me) * 2 + c_me
    partner = partners[0, 0]
    used = (partner >= 0).astype(F32)
    weight = jnp.where(own < partner, 1.0, -1.0).astype(F32) * used
    count = lax.dynamic_index_in_dim(counts, own, 0, keepdims=False)
    active = (jnp.arange(PAD, dtype=jnp.int32) < count).astype(F32)[:, None]
    shapes = jnp.pad(modes[0, 0], ((0, 2), (0, 0)))
    loads = jnp.pad(mode_loads[0], ((0, 2), (0, 0))) * active

    products = lax.dot_general(
        shapes,
        jnp.concatenate([shapes, gap[0, 0]], axis=0),
        (((1,), (1,)), ((), ())),
        precision=HIGHEST,
        preferred_element_type=F32,
    )
    lane = lanes((PAD, 128))
    tile = jnp.pad(
        jnp.concatenate([products[:, 0:8], loads, products[:, 8:16] * (weight * active)], axis=1),
        ((0, 0), (0, 104)),
    )
    tile = jnp.where(lane == 6, partner.astype(F32), tile)
    tile = jnp.where(lane == 7, count.astype(F32), tile)
    gathered = front_gather(jnp.concatenate([shapes, gap[0, 0], tile], axis=1))
    modes_all = jnp.stack([g[:, 0:M] for g in gathered])
    gap_all = jnp.stack([g[:, M:2 * M] for g in gathered])
    tiles = [g[:, 2 * M:] for g in gathered]
    packed = jnp.concatenate(
        [t[:, 0:8] for t in tiles]
        + [tiles[0][:, 8:16], tiles[0][:, 16:24] + tiles[1][:, 16:24] + tiles[2][:, 16:24] + tiles[3][:, 16:24]]
        + [jnp.zeros((PAD, 80), F32)],
        axis=1,
    )
    mates = jnp.stack([t[0, 6] for t in tiles]).astype(jnp.int32)
    weights = jnp.where(own < mates, 1.0, -1.0).astype(F32) * (mates >= 0).astype(F32)

    def place_of(sub):
        at = ((sub & 1) ^ c_me) * HALF + ((y_me - (sub >> 1)) & 3) * 8 + (sub >> 3)
        return jnp.where(sub >= 0, at, -1)

    me = jnp.concatenate([jnp.stack([c_me, y_me, z_me, x_me]), jnp.maximum(place_of(mates), 0)]).astype(jnp.int32)
    near, far = sub_gather(packed)
    heads = jnp.concatenate([near[:, 0, 6:8], far[:, 0, 6:8]], axis=0).astype(jnp.int32)
    mate_places = place_of(heads[:, 0])
    sub_counts = heads[:, 1]

    inverse, y_loads, y_gap = pl.pallas_call(
        coarse_kernel,
        out_shape=(sds(NP, NP), sds(4, NRHS, 128), sds(4, NRHS, 128)),
        in_specs=[SMEM, SMEM, VMEM, VMEM],
        out_specs=(VMEM, VMEM, VMEM),
        scratch_shapes=[pltpu.VMEM((NP, 128), F32), pltpu.VMEM((NP, NP), F32), pltpu.VMEM((BLK, BLK), F32)],
        compiler_params=PARAMS,
        name="coarse",
    )(sub_counts, me, near.reshape(NP // 2, 128), far.reshape(NP // 2, 128))

    panel_scratch = [pltpu.VMEM((4, M, M), BF16), pltpu.SemaphoreType.DMA((4,))]

    def exchange(payload, with_norm, name):
        return pl.pallas_call(
            functools.partial(mate_kernel, with_norm),
            out_shape=sds(NRHS, W_X),
            in_specs=[SMEM] * 4 + [ANY, ANY],
            out_specs=VMEM,
            scratch_shapes=[pltpu.VMEM((SUBS, NRHS, W_U), F32), pltpu.SemaphoreType.DMA((2,))],
            compiler_params=PARAMS,
            name=name,
        )(mate_places, sub_counts, me, weights, *sub_gather(payload))

    lam, payload = pl.pallas_call(
        begin_kernel,
        out_shape=(sds(NRHS, M), sds(NRHS, W_U)),
        in_specs=[SMEM, SMEM, VMEM, VMEM, ANY],
        out_specs=(VMEM, VMEM),
        scratch_shapes=panel_scratch,
        compiler_params=PARAMS,
        name="begin",
    )(me, weights, y_loads, modes_all, panels)

    xs = front_gather(exchange(payload, False, "mate_begin"))
    resid, direction, y_resid, payload = pl.pallas_call(
        first_kernel,
        out_shape=(sds(4, NRHS, M), sds(4, NRHS, M), sds(4, NRHS, 128), sds(NRHS, W_U)),
        in_specs=[SMEM, SMEM] + [VMEM] * 8 + [ANY],
        out_specs=(VMEM,) * 4,
        scratch_shapes=panel_scratch,
        compiler_params=PARAMS,
        name="first",
    )(me, weights, *xs, inverse, y_gap, gap_all, modes_all, panels)

    xs = front_gather(exchange(payload, True, "mate_first"))
    resid, direction, y_resid, lam, rho, payload = pl.pallas_call(
        second_kernel,
        out_shape=(sds(NRHS, M), sds(NRHS, M), sds(4, NRHS, 128), sds(NRHS, M), sds(NRHS, 128), sds(NRHS, W_U)),
        in_specs=[SMEM, SMEM] + [VMEM] * 10 + [ANY],
        out_specs=(VMEM,) * 6,
        scratch_shapes=panel_scratch,
        compiler_params=PARAMS,
        name="second",
    )(me, weights, *xs, inverse, y_resid, resid, direction, lam, modes_all, panels)

    xs = front_gather(exchange(payload, False, "mate_second"))
    lam, projected, _ = pl.pallas_call(
        last_kernel,
        out_shape=(sds(NRHS, M), sds(NRHS, M), sds(4, NRHS, 128)),
        in_specs=[SMEM, SMEM] + [VMEM] * 11,
        out_specs=(VMEM,) * 3,
        compiler_params=PARAMS,
        name="last",
    )(me, weights, *xs, inverse, y_resid, resid, direction, lam, rho, modes_all)
    return (lam[None, None], projected[None, None])


def solution(mesh):
    fine = Mesh(mesh.devices.reshape(8, 4, 2, 4), ("z", "y", "c", "x"))
    sub = ("z", "y", "c")
    in_specs = (
        P(sub, "x", None),
        P(sub, "x", None, None),
        P(sub, "x", None, None),
        P(sub, None, None),
        P(sub, "x"),
        P(),
    )
    out_specs = (P(sub, "x", None, None), P(sub, "x", None, None))
    return jax.shard_map(shards, mesh=fine, in_specs=in_specs, out_specs=out_specs, check_vma=False)
```

```python
import functools

import jax
import jax.numpy as jnp
from jax import lax
from jax.experimental import pallas as pl
from jax.experimental.pallas import tpu as pltpu
from jax.sharding import Mesh, PartitionSpec as P

MODES = 6
NRHS = 8
M = 768
SUBS = 64
PAD = 8
NP = SUBS * PAD
BLK = 128
HALF = SUBS // 2
HIGHEST = lax.Precision.HIGHEST
F32 = jnp.float32
BF16 = jnp.bfloat16

LANE_DU, LANE_ZZ, LANE_FF = 8, 9, 10
W_U = M + 128
W_X = M + NP + 128

SMEM = pl.BlockSpec(memory_space=pltpu.SMEM)
VMEM = pl.BlockSpec(memory_space=pltpu.VMEM)
ANY = pl.BlockSpec(memory_space=pl.ANY)
PARAMS = pltpu.CompilerParams(vmem_limit_bytes=40 * 1024 * 1024)


def lanes(shape):
    return lax.broadcasted_iota(jnp.int32, shape, len(shape) - 1)


def rows_of(shape):
    return lax.broadcasted_iota(jnp.int32, shape, 0)


def dot_high(a, b):
    return jnp.dot(a, b, precision=HIGHEST, preferred_element_type=F32)


def split(x):
    high = x.astype(BF16).astype(F32)
    rest = x - high
    middle = rest.astype(BF16).astype(F32)
    return high, middle, rest - middle


def dot_six(a, b):
    ah, am, al = (p.astype(BF16) for p in split(a))
    bh, bm, bl = (p.astype(BF16) for p in split(b))
    left = jnp.concatenate([ah, am, ah, am, ah, al], axis=1)
    right = jnp.concatenate([bh, bh, bm, bm, bl, bh], axis=0)
    return jnp.dot(left, right, preferred_element_type=F32)


def dot_pieces(a, pieces_ref):
    stacked = jnp.concatenate(split(a), axis=0)
    rows = a.shape[0]
    part = jnp.dot(stacked.astype(BF16), pieces_ref[0], preferred_element_type=F32)
    total = part[0:rows] + part[rows:2 * rows] + part[2 * rows:3 * rows]
    part = jnp.dot(stacked[0:2 * rows].astype(BF16), pieces_ref[1], preferred_element_type=F32)
    total = total + (part[0:rows] + part[rows:2 * rows])
    return total + jnp.dot(stacked[0:rows].astype(BF16), pieces_ref[2], preferred_element_type=F32)


def coarse_kernel(cnt_ref, me_ref, own_ref, oth_ref, inv_ref, y0_ref, yg_ref, g_ref, a_ref, d_ref):
    g_ref[0:NP // 2, :] = own_ref[...]
    g_ref[NP // 2:NP, :] = oth_ref[...]
    core, y_me = me_ref[0], me_ref[1]
    row_1 = rows_of((BLK, 1))
    lane = lanes((BLK, BLK))
    col_1 = lanes((1, NP))
    flipped = g_ref[...].T
    col_active = (lax.bitwise_and(col_1, 7) < flipped[7:8, :].astype(jnp.int32)).astype(F32)
    for b in range(NP // BLK):
        rows = g_ref[b * BLK:(b + 1) * BLK, :]
        row_id = row_1 + b * BLK
        row_sub = lax.shift_right_logical(row_id, 3)
        row_active = (lax.bitwise_and(row_id, 7) < rows[:, 7:8].astype(jnp.int32)).astype(F32)
        grams, places = [], []
        for k in range(4):
            mate = rows[:, 8 * k + 6:8 * k + 7].astype(jnp.int32)
            place = (
                lax.bitwise_xor(lax.bitwise_and(mate, 1), core) * HALF
                + lax.bitwise_and(y_me - lax.shift_right_logical(mate, 1), 3) * 8
                + lax.shift_right_logical(mate, 3)
            )
            gram = rows if k == 0 else pltpu.roll(rows, BLK - 8 * k, 1)
            gram = jnp.where(lane < MODES, gram, 0.0) * ((mate >= 0).astype(F32) * row_active)
            for step in (8, 16, 32, 64):
                gram = gram + pltpu.roll(gram, step, 1)
            grams.append(gram)
            places.append(place)
        whole = grams[0] + grams[1] + grams[2] + grams[3]
        for t in range(NP // BLK):
            col_id = lane + t * BLK
            col_sub = lax.shift_right_logical(col_id, 3)
            total = jnp.where(row_sub == col_sub, whole, 0.0)
            for k in range(4):
                total = total - jnp.where(places[k] == col_sub, grams[k], 0.0)
            total = total * col_active[:, t * BLK:(t + 1) * BLK]
            total = total + jnp.where(row_id == col_id, 1.0 - row_active, 0.0)
            a_ref[b * BLK:(b + 1) * BLK, t * BLK:(t + 1) * BLK] = total

    tile_lane = lanes((PAD, BLK))
    tile_row = rows_of((PAD, BLK))

    def sweep(i, pivots):
        p = PAD * i
        rows = d_ref[p:p + PAD, :]
        columns = [jnp.broadcast_to(rows[:, p + b:p + b + 1], (PAD, BLK)) for b in range(pivots)]
        s = [[None] * pivots for _ in range(pivots)]
        for b in range(pivots):
            for a in range(b + 1):
                s[a][b] = jnp.broadcast_to(columns[b][a:a + 1, :], (PAD, BLK))
        for v in range(pivots):
            over = 1.0 / s[v][v]
            line = [s[min(v, b)][max(v, b)] for b in range(pivots)]
            scaled = [x * over for x in line]
            for a in range(pivots):
                for b in range(a, pivots):
                    if a != v and b != v:
                        s[a][b] = s[a][b] - line[a] * scaled[b]
            for b in range(pivots):
                if b != v:
                    s[min(v, b)][max(v, b)] = scaled[b]
            s[v][v] = -over
        new_rows = jnp.zeros((PAD, BLK), F32)
        tails = []
        for b in range(pivots):
            column = jnp.zeros((PAD, BLK), F32)
            for a in range(pivots):
                column = jnp.where(tile_row == a, s[min(a, b)][max(a, b)], column)
            new_rows = new_rows - column * rows[b:b + 1, :]
            tails.append(column)
        for b in range(pivots):
            new_rows = jnp.where(tile_lane == p + b, tails[b], new_rows)
        mat = d_ref[...]
        new = jnp.where((lane >= p) & (lane < p + pivots), 0.0, mat)
        for b in range(pivots):
            new = new - mat[:, p + b:p + b + 1] * new_rows[b:b + 1, :]
        d_ref[...] = new
        d_ref[p:p + PAD, :] = jnp.where(tile_row < pivots, new_rows, rows)

    for b in range(NP // BLK):
        lo, hi = b * BLK, (b + 1) * BLK
        d_ref[...] = a_ref[lo:hi, lo:hi]

        for i in range(BLK // PAD):
            count = cnt_ref[b * (BLK // PAD) + i]
            for low, high in ((1, 3), (4, 6)):
                @pl.when((count >= low) & (count <= high))
                def _(i=i, high=high):
                    sweep(i, high)

        small = -d_ref[...]
        tall = a_ref[:, lo:hi]
        wide = dot_six(small, a_ref[lo:hi, :])
        a_ref[...] = a_ref[...] - dot_six(tall, wide)
        a_ref[:, lo:hi] = dot_six(tall, small)
        a_ref[lo:hi, :] = wide
        a_ref[lo:hi, lo:hi] = -small
    pieces = split(-a_ref[...])
    for n in range(3):
        inv_ref[n] = pieces[n].astype(BF16)
    y = dot_pieces(flipped[32:48, :], inv_ref)
    for b in range(NP // BLK):
        y0_ref[b] = y[0:8, b * BLK:(b + 1) * BLK]
        yg_ref[b] = y[8:16, b * BLK:(b + 1) * BLK]


def mate_kernel(with_norm, mate_ref, cnt_ref, me_ref, w_ref, own_ref, oth_ref, out_ref, g_ref, sems):
    first = pltpu.make_async_copy(own_ref, g_ref.at[0:HALF], sems.at[0])
    second = pltpu.make_async_copy(oth_ref, g_ref.at[HALF:SUBS], sems.at[1])
    first.start()
    second.start()
    first.wait()
    second.wait()
    mine = me_ref[2]
    theirs = jnp.maximum(mate_ref[mine], 0)
    out_ref[:, 0:M] = w_ref[0] * (g_ref[mine][:, 0:M] - g_ref[theirs][:, 0:M])
    lane = lanes((NRHS, 128))
    sums = [jnp.zeros((NRHS, 128), F32) for _ in range(NP // BLK)]
    scalars = jnp.zeros((NRHS, 128), F32)
    norm = jnp.zeros((NRHS, M), F32)
    for p in range(SUBS):
        mate = mate_ref[p]
        used = (mate >= 0).astype(F32)
        at = jnp.maximum(mate, 0)
        tile = g_ref[p, :, M:W_U]
        scalars = scalars + tile
        limit = jnp.where(mate >= 0, cnt_ref[p], 0)
        piece = jnp.where(lane < limit, tile - g_ref[at, :, M:W_U], 0.0)
        if p % 16:
            piece = pltpu.roll(piece, 8 * (p % 16), 1)
        sums[p // 16] = sums[p // 16] + piece
        if with_norm:
            gone = g_ref[p, :, 0:M] - g_ref[at, :, 0:M]
            norm = norm + used * (gone * gone)
    for b in range(NP // BLK):
        out_ref[:, M + b * BLK:M + (b + 1) * BLK] = sums[b]
    if with_norm:
        scalars = jnp.where(lane == LANE_FF, 0.5 * jnp.sum(norm, axis=1, keepdims=True), scalars)
    out_ref[:, M + NP:W_X] = scalars


def y_at(y_ref, place):
    tile = y_ref[lax.div(place, 16)]
    return pltpu.roll(tile, lax.rem(128 - 8 * lax.rem(place, 16), 128), 1)


def expand(y_ref, me_ref, w_ref, modes_ref, k):
    coeff = y_at(y_ref, me_ref[2]) - y_at(y_ref, me_ref[4 + k])
    total = coeff[:, 0:1] * modes_ref[k, 0:1, :]
    for m in range(1, MODES):
        total = total + coeff[:, m:m + 1] * modes_ref[k, m:m + 1, :]
    return w_ref[k] * total


def start_panel(me_ref, panel_ref, pan_ref, sems):
    copies = []
    for k in range(4):
        at = pl.multiple_of(lax.bitwise_and(me_ref[3] - k, 3) * M, M)
        copy = pltpu.make_async_copy(panel_ref.at[0, :, pl.ds(at, M)], pan_ref.at[k], sems.at[k])
        copy.start()
        copies.append(copy)
    return copies


def apply_panel(copies, w_ref, modes_ref, vectors, pan_ref, pay_ref, square):
    total = None
    for k in range(4):
        load = (w_ref[k] * vectors[k]).astype(BF16)
        copies[k].wait()
        part = lax.dot_general(load, pan_ref[k], (((1,), (1,)), ((), ())), preferred_element_type=F32)
        total = part if total is None else total + part
    lane = lanes((NRHS, 128))
    tail = jnp.zeros((NRHS, 128), F32)
    for m in range(MODES):
        tail = jnp.where(lane == m, jnp.sum(total * modes_ref[0, m:m + 1, :], axis=1, keepdims=True), tail)
    dots = jnp.sum(w_ref[0] * vectors[0] * total, axis=1, keepdims=True)
    tail = jnp.where(lane == LANE_DU, dots, tail)
    if square is not None:
        tail = jnp.where(lane == LANE_ZZ, 0.5 * jnp.sum(square * square, axis=1, keepdims=True), tail)
    pay_ref[:, 0:M] = total
    pay_ref[:, M:W_U] = tail


def begin_kernel(me_ref, w_ref, y_ref, modes_ref, panel_ref, lam_ref, pay_ref, pan_ref, sems):
    copies = start_panel(me_ref, panel_ref, pan_ref, sems)
    vectors = [expand(y_ref, me_ref, w_ref, modes_ref, k) for k in range(4)]
    lam_ref[...] = vectors[0]
    apply_panel(copies, w_ref, modes_ref, vectors, pan_ref, pay_ref, None)


def gathered_sums(x_refs, inv_ref):
    ms = x_refs[0][:, M:M + NP]
    scalars = x_refs[0][:, M + NP:W_X]
    for ref in x_refs[1:]:
        ms = ms + ref[:, M:M + NP]
        scalars = scalars + ref[:, M + NP:W_X]
    return ms, dot_pieces(ms, inv_ref), scalars


def first_kernel(me_ref, w_ref, x0, x1, x2, x3, inv_ref, yg_ref, gap_ref, modes_ref, panel_ref,
                 r_ref, z_ref, y_ref, pay_ref, pan_ref, sems):
    copies = start_panel(me_ref, panel_ref, pan_ref, sems)
    xs = (x0, x1, x2, x3)
    _, solved, _ = gathered_sums(xs, inv_ref)
    for b in range(NP // BLK):
        y_ref[b] = yg_ref[b] - solved[:, b * BLK:(b + 1) * BLK]
    vectors = []
    for k in range(4):
        resid = w_ref[k] * w_ref[k] * gap_ref[k] - xs[k][:, 0:M]
        r_ref[k] = resid
        z = resid - expand(y_ref, me_ref, w_ref, modes_ref, k)
        z_ref[k] = z
        vectors.append(z)
    apply_panel(copies, w_ref, modes_ref, vectors, pan_ref, pay_ref, vectors[0])


def second_kernel(me_ref, w_ref, x0, x1, x2, x3, inv_ref, y_ref, r_ref, d_ref, lam_ref, modes_ref, panel_ref,
                  r_out, d_out, y_out, lam_out, rho_out, pay_ref, pan_ref, sems):
    copies = start_panel(me_ref, panel_ref, pan_ref, sems)
    xs = (x0, x1, x2, x3)
    ms, solved, scalars = gathered_sums(xs, inv_ref)
    rho = scalars[:, LANE_ZZ:LANE_ZZ + 1]
    alpha = rho / scalars[:, LANE_DU:LANE_DU + 1]
    squared = scalars[:, LANE_FF:LANE_FF + 1] - jnp.sum(ms * solved, axis=1, keepdims=True)
    rho_new = jnp.maximum(alpha * alpha * squared - rho, 0.0)
    beta = rho_new / rho
    for b in range(NP // BLK):
        y_out[b] = y_ref[b] - alpha * solved[:, b * BLK:(b + 1) * BLK]
    vectors = []
    for k in range(4):
        resid = r_ref[k] - alpha * xs[k][:, 0:M]
        direction = resid - expand(y_out, me_ref, w_ref, modes_ref, k) + beta * d_ref[k]
        vectors.append(direction)
        if k == 0:
            r_out[...] = resid
            d_out[...] = direction
    lam_out[...] = lam_ref[...] + alpha * d_ref[0]
    rho_out[...] = jnp.broadcast_to(rho_new, (NRHS, 128))
    apply_panel(copies, w_ref, modes_ref, vectors, pan_ref, pay_ref, None)


def last_kernel(me_ref, w_ref, x0, x1, x2, x3, inv_ref, y_ref, r_ref, d_ref, lam_ref, rho_ref, modes_ref,
                lam_out, z_out, y_out):
    xs = (x0, x1, x2, x3)
    _, solved, scalars = gathered_sums(xs, inv_ref)
    alpha = rho_ref[:, 0:1] / scalars[:, LANE_DU:LANE_DU + 1]
    for b in range(NP // BLK):
        y_out[b] = y_ref[b] - alpha * solved[:, b * BLK:(b + 1) * BLK]
    resid = r_ref[...] - alpha * x0[:, 0:M]
    lam_out[...] = lam_ref[...] + alpha * d_ref[...]
    z_out[...] = resid - expand(y_out, me_ref, w_ref, modes_ref, 0)


def shift(value, axis, step):
    size = lax.axis_size(axis)
    return lax.ppermute(value, axis, [(i, (i + step) % size) for i in range(size)])


def front_gather(value):
    return [value] + [shift(value, "x", k) for k in range(1, 4)]


def sub_gather(value):
    width = value.shape[-1]
    copies = jnp.broadcast_to(value[None], (8,) + value.shape)
    along_z = lax.all_to_all(copies, "z", 0, 0, tiled=True)
    own = jnp.concatenate([along_z] + [shift(along_z, "y", k) for k in range(1, 4)], axis=0)
    other = shift(own, "c", 1)
    return own.reshape(HALF, NRHS, width), other.reshape(HALF, NRHS, width)


def sds(*shape):
    return jax.ShapeDtypeStruct(shape, F32)


def coarse_call(sub_counts, me, near, far):
    return pl.pallas_call(
        coarse_kernel,
        out_shape=(jax.ShapeDtypeStruct((3, NP, NP), BF16), sds(4, NRHS, 128), sds(4, NRHS, 128)),
        in_specs=[SMEM, SMEM, VMEM, VMEM],
        out_specs=(VMEM, VMEM, VMEM),
        scratch_shapes=[pltpu.VMEM((NP, 128), F32), pltpu.VMEM((NP, NP), F32), pltpu.VMEM((BLK, BLK), F32)],
        compiler_params=PARAMS,
        name="coarse",
    )(sub_counts, me, near, far)


def shards(panels, gap, modes, mode_loads, partners, counts):
    z_me, y_me, c_me, x_me = (lax.axis_index(a) for a in ("z", "y", "c", "x"))
    own = (z_me * 4 + y_me) * 2 + c_me
    partner = partners[0, 0]
    used = (partner >= 0).astype(F32)
    weight = jnp.where(own < partner, 1.0, -1.0).astype(F32) * used
    count = lax.dynamic_index_in_dim(counts, own, 0, keepdims=False)
    active = (jnp.arange(PAD, dtype=jnp.int32) < count).astype(F32)[:, None]
    shapes = jnp.pad(modes[0, 0], ((0, 2), (0, 0)))
    loads = jnp.pad(mode_loads[0], ((0, 2), (0, 0))) * active

    products = lax.dot_general(
        shapes,
        jnp.concatenate([shapes, gap[0, 0]], axis=0),
        (((1,), (1,)), ((), ())),
        precision=HIGHEST,
        preferred_element_type=F32,
    )
    lane = lanes((PAD, 128))
    tile = jnp.pad(
        jnp.concatenate([products[:, 0:8], loads, products[:, 8:16] * (weight * active)], axis=1),
        ((0, 0), (0, 104)),
    )
    tile = jnp.where(lane == 6, partner.astype(F32), tile)
    tile = jnp.where(lane == 7, count.astype(F32), tile)
    gathered = front_gather(jnp.concatenate([shapes, gap[0, 0], tile], axis=1))
    modes_all = jnp.stack([g[:, 0:M] for g in gathered])
    gap_all = jnp.stack([g[:, M:2 * M] for g in gathered])
    tiles = [g[:, 2 * M:] for g in gathered]
    packed = jnp.concatenate(
        [t[:, 0:8] for t in tiles]
        + [tiles[0][:, 8:16], tiles[0][:, 16:24] + tiles[1][:, 16:24] + tiles[2][:, 16:24] + tiles[3][:, 16:24]]
        + [jnp.zeros((PAD, 80), F32)],
        axis=1,
    )
    mates = jnp.stack([t[0, 6] for t in tiles]).astype(jnp.int32)
    weights = jnp.where(own < mates, 1.0, -1.0).astype(F32) * (mates >= 0).astype(F32)

    def place_of(sub):
        at = ((sub & 1) ^ c_me) * HALF + ((y_me - (sub >> 1)) & 3) * 8 + (sub >> 3)
        return jnp.where(sub >= 0, at, -1)

    me = jnp.concatenate([jnp.stack([c_me, y_me, z_me, x_me]), jnp.maximum(place_of(mates), 0)]).astype(jnp.int32)
    near, far = sub_gather(packed)
    heads = jnp.concatenate([near[:, 0, 6:8], far[:, 0, 6:8]], axis=0).astype(jnp.int32)
    mate_places = place_of(heads[:, 0])
    sub_counts = heads[:, 1]

    inverse, y_loads, y_gap = coarse_call(
        sub_counts, me, near.reshape(NP // 2, 128), far.reshape(NP // 2, 128)
    )

    panel_scratch = [pltpu.VMEM((4, M, M), BF16), pltpu.SemaphoreType.DMA((4,))]

    def exchange(payload, with_norm, name):
        return pl.pallas_call(
            functools.partial(mate_kernel, with_norm),
            out_shape=sds(NRHS, W_X),
            in_specs=[SMEM] * 4 + [ANY, ANY],
            out_specs=VMEM,
            scratch_shapes=[pltpu.VMEM((SUBS, NRHS, W_U), F32), pltpu.SemaphoreType.DMA((2,))],
            compiler_params=PARAMS,
            name=name,
        )(mate_places, sub_counts, me, weights, *sub_gather(payload))

    lam, payload = pl.pallas_call(
        begin_kernel,
        out_shape=(sds(NRHS, M), sds(NRHS, W_U)),
        in_specs=[SMEM, SMEM, VMEM, VMEM, ANY],
        out_specs=(VMEM, VMEM),
        scratch_shapes=panel_scratch,
        compiler_params=PARAMS,
        name="begin",
    )(me, weights, y_loads, modes_all, panels)

    xs = front_gather(exchange(payload, False, "mate_begin"))
    resid, direction, y_resid, payload = pl.pallas_call(
        first_kernel,
        out_shape=(sds(4, NRHS, M), sds(4, NRHS, M), sds(4, NRHS, 128), sds(NRHS, W_U)),
        in_specs=[SMEM, SMEM] + [VMEM] * 8 + [ANY],
        out_specs=(VMEM,) * 4,
        scratch_shapes=panel_scratch,
        compiler_params=PARAMS,
        name="first",
    )(me, weights, *xs, inverse, y_gap, gap_all, modes_all, panels)

    xs = front_gather(exchange(payload, True, "mate_first"))
    resid, direction, y_resid, lam, rho, payload = pl.pallas_call(
        second_kernel,
        out_shape=(sds(NRHS, M), sds(NRHS, M), sds(4, NRHS, 128), sds(NRHS, M), sds(NRHS, 128), sds(NRHS, W_U)),
        in_specs=[SMEM, SMEM] + [VMEM] * 10 + [ANY],
        out_specs=(VMEM,) * 6,
        scratch_shapes=panel_scratch,
        compiler_params=PARAMS,
        name="second",
    )(me, weights, *xs, inverse, y_resid, resid, direction, lam, modes_all, panels)

    xs = front_gather(exchange(payload, False, "mate_second"))
    lam, projected, _ = pl.pallas_call(
        last_kernel,
        out_shape=(sds(NRHS, M), sds(NRHS, M), sds(4, NRHS, 128)),
        in_specs=[SMEM, SMEM] + [VMEM] * 11,
        out_specs=(VMEM,) * 3,
        compiler_params=PARAMS,
        name="last",
    )(me, weights, *xs, inverse, y_resid, resid, direction, lam, rho, modes_all)
    return (lam[None, None], projected[None, None])


def solution(mesh):
    fine = Mesh(mesh.devices.reshape(8, 4, 2, 4), ("z", "y", "c", "x"))
    sub = ("z", "y", "c")
    in_specs = (
        P(sub, "x", None),
        P(sub, "x", None, None),
        P(sub, "x", None, None),
        P(sub, None, None),
        P(sub, "x"),
        P(),
    )
    out_specs = (P(sub, "x", None, None), P(sub, "x", None, None))
    return jax.shard_map(shards, mesh=fine, in_specs=in_specs, out_specs=out_specs, check_vma=False)
```

```python
import functools

import jax
import jax.numpy as jnp
from jax import lax
from jax.experimental import pallas as pl
from jax.experimental.pallas import tpu as pltpu
from jax.sharding import Mesh, PartitionSpec as P

MODES = 6
NRHS = 8
M = 768
SUBS = 64
PAD = 8
NP = SUBS * PAD
BLK = 128
HALF = SUBS // 2
HIGHEST = lax.Precision.HIGHEST
F32 = jnp.float32
BF16 = jnp.bfloat16

LANE_DU, LANE_ZZ, LANE_FF = 6, 7, 8
W_U = M + 128
W_X = M + NP + 128

SMEM = pl.BlockSpec(memory_space=pltpu.SMEM)
VMEM = pl.BlockSpec(memory_space=pltpu.VMEM)
ANY = pl.BlockSpec(memory_space=pl.ANY)
PARAMS = pltpu.CompilerParams(vmem_limit_bytes=16 * 1024 * 1024)


def lanes(shape):
    return lax.broadcasted_iota(jnp.int32, shape, len(shape) - 1)


def rows_of(shape):
    return lax.broadcasted_iota(jnp.int32, shape, 0)


def dot_high(a, b):
    return jnp.dot(a, b, precision=HIGHEST, preferred_element_type=F32)


def split(x):
    high = x.astype(BF16).astype(F32)
    rest = x - high
    middle = rest.astype(BF16).astype(F32)
    return high, middle, rest - middle


def dot_six(a, b):
    ah, am, al = (p.astype(BF16) for p in split(a))
    bh, bm, bl = (p.astype(BF16) for p in split(b))
    left = jnp.concatenate([ah, am, ah, am, ah, al], axis=1)
    right = jnp.concatenate([bh, bh, bm, bm, bl, bh], axis=0)
    return jnp.dot(left, right, preferred_element_type=F32)


def dot_pieces(a, pieces_ref):
    stacked = jnp.concatenate(split(a), axis=0)
    rows = a.shape[0]
    part = jnp.dot(stacked.astype(BF16), pieces_ref[0], preferred_element_type=F32)
    total = part[0:rows] + part[rows:2 * rows] + part[2 * rows:3 * rows]
    part = jnp.dot(stacked[0:2 * rows].astype(BF16), pieces_ref[1], preferred_element_type=F32)
    total = total + (part[0:rows] + part[rows:2 * rows])
    return total + jnp.dot(stacked[0:rows].astype(BF16), pieces_ref[2], preferred_element_type=F32)


def coarse_kernel(cnt_ref, me_ref, w_ref, g_ref, modes_ref, panel_ref,
                  inv_ref, yg_ref, lam_ref, pay_ref, a_ref, d_ref, y0_ref, held_ref, sem):
    copy = pltpu.make_async_copy(panel_ref, held_ref, sem)
    copy.start()
    row_1 = rows_of((BLK, 1))
    lane = lanes((BLK, BLK))
    col_1 = lanes((1, NP))
    flipped = g_ref[...].T
    col_active = (lax.bitwise_and(col_1, 7) < flipped[7:8, :].astype(jnp.int32)).astype(F32)
    for b in range(NP // BLK):
        rows = g_ref[b * BLK:(b + 1) * BLK, :]
        row_id = row_1 + b * BLK
        row_sub = lax.shift_right_logical(row_id, 3)
        row_active = (lax.bitwise_and(row_id, 7) < rows[:, 7:8].astype(jnp.int32)).astype(F32)
        grams, places = [], []
        for k in range(4):
            mate = rows[:, 8 * k + 6:8 * k + 7].astype(jnp.int32)
            place = lax.bitwise_and(mate, 7) * 8 + lax.shift_right_logical(mate, 3)
            gram = rows if k == 0 else pltpu.roll(rows, BLK - 8 * k, 1)
            gram = jnp.where(lane < MODES, gram, 0.0) * ((mate >= 0).astype(F32) * row_active)
            for step in (8, 16, 32, 64):
                gram = gram + pltpu.roll(gram, step, 1)
            grams.append(gram)
            places.append(place)
        whole = grams[0] + grams[1] + grams[2] + grams[3]
        for t in range(NP // BLK):
            col_id = lane + t * BLK
            col_sub = lax.shift_right_logical(col_id, 3)
            total = jnp.where(row_sub == col_sub, whole, 0.0)
            for k in range(4):
                total = total - jnp.where(places[k] == col_sub, grams[k], 0.0)
            total = total * col_active[:, t * BLK:(t + 1) * BLK]
            total = total + jnp.where(row_id == col_id, 1.0 - row_active, 0.0)
            a_ref[b * BLK:(b + 1) * BLK, t * BLK:(t + 1) * BLK] = total

    tile_lane = lanes((PAD, BLK))
    tile_row = rows_of((PAD, BLK))

    def sweep(i, pivots):
        p = PAD * i
        rows = d_ref[p:p + PAD, :]
        columns = [jnp.broadcast_to(rows[:, p + b:p + b + 1], (PAD, BLK)) for b in range(pivots)]
        s = [[None] * pivots for _ in range(pivots)]
        for b in range(pivots):
            for a in range(b + 1):
                s[a][b] = jnp.broadcast_to(columns[b][a:a + 1, :], (PAD, BLK))
        for v in range(pivots):
            over = 1.0 / s[v][v]
            line = [s[min(v, b)][max(v, b)] for b in range(pivots)]
            scaled = [x * over for x in line]
            for a in range(pivots):
                for b in range(a, pivots):
                    if a != v and b != v:
                        s[a][b] = s[a][b] - line[a] * scaled[b]
            for b in range(pivots):
                if b != v:
                    s[min(v, b)][max(v, b)] = scaled[b]
            s[v][v] = -over
        new_rows = jnp.zeros((PAD, BLK), F32)
        tails = []
        for b in range(pivots):
            column = jnp.zeros((PAD, BLK), F32)
            for a in range(pivots):
                column = jnp.where(tile_row == a, s[min(a, b)][max(a, b)], column)
            new_rows = new_rows - column * rows[b:b + 1, :]
            tails.append(column)
        for b in range(pivots):
            new_rows = jnp.where(tile_lane == p + b, tails[b], new_rows)
        mat = d_ref[...]
        new = jnp.where((lane >= p) & (lane < p + pivots), 0.0, mat)
        for b in range(pivots):
            new = new - mat[:, p + b:p + b + 1] * new_rows[b:b + 1, :]
        d_ref[...] = new
        d_ref[p:p + PAD, :] = jnp.where(tile_row < pivots, new_rows, rows)

    for b in range(NP // BLK):
        lo, hi = b * BLK, (b + 1) * BLK
        d_ref[...] = a_ref[lo:hi, lo:hi]

        for i in range(BLK // PAD):
            count = cnt_ref[b * (BLK // PAD) + i]
            for low, high in ((1, 3), (4, 6)):
                @pl.when((count >= low) & (count <= high))
                def _(i=i, high=high):
                    sweep(i, high)

        small = -d_ref[...]
        tall = a_ref[:, lo:hi]
        wide = dot_six(small, a_ref[lo:hi, :])
        a_ref[...] = a_ref[...] - dot_six(tall, wide)
        a_ref[:, lo:hi] = dot_six(tall, small)
        a_ref[lo:hi, :] = wide
        a_ref[lo:hi, lo:hi] = -small
    pieces = split(-a_ref[...])
    for n in range(3):
        inv_ref[n] = pieces[n].astype(BF16)
    y = dot_pieces(flipped[32:48, :], inv_ref)
    for b in range(NP // BLK):
        y0_ref[b] = y[0:8, b * BLK:(b + 1) * BLK]
        yg_ref[b] = y[8:16, b * BLK:(b + 1) * BLK]
    vectors = [expand(y0_ref, me_ref, w_ref, modes_ref, k) for k in range(4)]
    lam_ref[...] = vectors[0]
    copy.wait()
    apply_panel(me_ref, w_ref, modes_ref, vectors, held_ref, pay_ref, None)


def mate_kernel(mate_ref, cnt_ref, me_ref, w_ref, own_ref, oth_ref, out_ref, g_ref, sems):
    first = pltpu.make_async_copy(own_ref, g_ref.at[0:HALF], sems.at[0])
    second = pltpu.make_async_copy(oth_ref, g_ref.at[HALF:SUBS], sems.at[1])
    first.start()
    second.start()
    first.wait()
    second.wait()
    core, y_me = me_ref[0], me_ref[1]

    def held(place):
        group = lax.shift_right_logical(place, 3)
        apart = lax.bitwise_and(y_me - lax.shift_right_logical(group, 1), 3)
        return lax.bitwise_xor(lax.bitwise_and(group, 1), core) * HALF + apart * 8 + lax.bitwise_and(place, 7)

    mine = held(me_ref[2])
    theirs = held(me_ref[4])
    out_ref[:, 0:M] = w_ref[0] * (g_ref[mine][:, 0:M] - g_ref[theirs][:, 0:M])
    lane = lanes((NRHS, 128))
    sums = [jnp.zeros((NRHS, 128), F32) for _ in range(NP // BLK)]
    scalars = jnp.zeros((NRHS, 128), F32)
    norm = jnp.zeros((NRHS, M), F32)
    for p in range(SUBS):
        mate = mate_ref[p]
        used = (mate >= 0).astype(F32)
        here = held(jnp.int32(p))
        at = held(jnp.maximum(mate, 0))
        tile = g_ref[here, :, M:W_U]
        scalars = scalars + tile
        limit = jnp.where(mate >= 0, cnt_ref[p], 0)
        piece = jnp.where(lane < limit, tile - g_ref[at, :, M:W_U], 0.0)
        if p % 16:
            piece = pltpu.roll(piece, 8 * (p % 16), 1)
        sums[p // 16] = sums[p // 16] + piece
        gone = g_ref[here, :, 0:M] - g_ref[at, :, 0:M]
        norm = norm + used * (gone * gone)
    for b in range(NP // BLK):
        out_ref[:, M + b * BLK:M + (b + 1) * BLK] = sums[b]
    scalars = jnp.where(lane == LANE_FF, 0.5 * jnp.sum(norm, axis=1, keepdims=True), scalars)
    out_ref[:, M + NP:W_X] = scalars


def choose_kernel(mate_ref, me_ref, z_ref, out_ref):
    lane = lanes((NRHS, 128))
    tail = jnp.where(lane < 8, z_ref[0, :, M:W_U], 0.0)
    for z in range(1, 8):
        tail = tail + pltpu.roll(jnp.where(lane < 8, z_ref[z, :, M:W_U], 0.0), 8 * z, 1)
    for group in range(8):
        mate = jnp.maximum(mate_ref[group * 8 + lax.bitwise_and(me_ref[2], 7)], 0)
        out_ref[group, :, 0:M] = z_ref[lax.bitwise_and(mate, 7), :, 0:M]
        out_ref[group, :, M:W_U] = tail


def match_kernel(mate_ref, cnt_ref, me_ref, w_ref, own_ref, got_ref, img_ref, sum_ref, q_ref):
    theirs = lax.shift_right_logical(me_ref[4], 3)
    img_ref[...] = w_ref[0] * (own_ref[:, 0:M] - got_ref[theirs][:, 0:M])
    lane = lanes((NRHS, 128))
    scalars = jnp.zeros((NRHS, 128), F32)
    for b in range(NP // BLK):
        both = got_ref[2 * b, :, M:W_U] + pltpu.roll(got_ref[2 * b + 1, :, M:W_U], 64, 1)
        q_ref[b] = both
        scalars = scalars + both
    for step in (8, 16, 32, 64):
        scalars = scalars + pltpu.roll(scalars, step, 1)
    for b in range(NP // BLK):
        total = jnp.zeros((NRHS, 128), F32)
        here = q_ref[b]
        for i in range(16):
            p = b * 16 + i
            mate = mate_ref[p]
            at = jnp.maximum(mate, 0)
            step = lax.bitwise_and(8 * (i - at), 127)
            there = pltpu.roll(q_ref[lax.shift_right_logical(at, 4)], step, 1)
            limit = 8 * i + jnp.where(mate >= 0, cnt_ref[p], 0)
            total = jnp.where((lane >= 8 * i) & (lane < limit), here - there, total)
        sum_ref[:, b * BLK:(b + 1) * BLK] = total
    sum_ref[:, NP:NP + 128] = scalars


def y_at(y_ref, place):
    tile = y_ref[lax.div(place, 16)]
    return pltpu.roll(tile, lax.rem(128 - 8 * lax.rem(place, 16), 128), 1)


def expand(y_ref, me_ref, w_ref, modes_ref, k):
    coeff = y_at(y_ref, me_ref[2]) - y_at(y_ref, me_ref[4 + k])
    total = coeff[:, 0:1] * modes_ref[k, 0:1, :]
    for m in range(1, MODES):
        total = total + coeff[:, m:m + 1] * modes_ref[k, m:m + 1, :]
    return w_ref[k] * total


def apply_panel(me_ref, w_ref, modes_ref, vectors, panel_ref, pay_ref, square):
    total = None
    for k in range(4):
        load = (w_ref[k] * vectors[k]).astype(BF16)
        at = pl.multiple_of(lax.bitwise_and(me_ref[3] - k, 3) * M, M)
        slot = panel_ref[0, :, pl.ds(at, M)]
        part = lax.dot_general(load, slot, (((1,), (1,)), ((), ())), preferred_element_type=F32)
        total = part if total is None else total + part
    lane = lanes((NRHS, 128))
    tail = jnp.zeros((NRHS, 128), F32)
    for m in range(MODES):
        tail = jnp.where(lane == m, jnp.sum(total * modes_ref[0, m:m + 1, :], axis=1, keepdims=True), tail)
    dots = jnp.sum(w_ref[0] * vectors[0] * total, axis=1, keepdims=True)
    tail = jnp.where(lane == LANE_DU, dots, tail)
    if square is not None:
        tail = jnp.where(lane == LANE_ZZ, 0.5 * jnp.sum(square * square, axis=1, keepdims=True), tail)
    pay_ref[:, 0:M] = total
    pay_ref[:, M:W_U] = tail


def gathered_sums(x_refs, inv_ref, at=M):
    ms = x_refs[0][:, at:at + NP]
    scalars = x_refs[0][:, at + NP:at + NP + 128]
    for ref in x_refs[1:]:
        ms = ms + ref[:, at:at + NP]
        scalars = scalars + ref[:, at + NP:at + NP + 128]
    return ms, dot_pieces(ms, inv_ref), scalars


def first_kernel(me_ref, w_ref, x0, x1, x2, x3, inv_ref, yg_ref, gap_ref, modes_ref, panel_ref,
                 r_ref, z_ref, y_ref, pay_ref):
    xs = (x0, x1, x2, x3)
    _, solved, _ = gathered_sums(xs, inv_ref)
    for b in range(NP // BLK):
        y_ref[b] = yg_ref[b] - solved[:, b * BLK:(b + 1) * BLK]
    vectors = []
    for k in range(4):
        resid = w_ref[k] * w_ref[k] * gap_ref[k] - xs[k][:, 0:M]
        r_ref[k] = resid
        z = resid - expand(y_ref, me_ref, w_ref, modes_ref, k)
        z_ref[k] = z
        vectors.append(z)
    apply_panel(me_ref, w_ref, modes_ref, vectors, panel_ref, pay_ref, vectors[0])


def second_kernel(me_ref, w_ref, x0, x1, x2, x3, inv_ref, y_ref, r_ref, d_ref, lam_ref, modes_ref, panel_ref,
                  r_out, d_out, y_out, lam_out, rho_out, pay_ref):
    xs = (x0, x1, x2, x3)
    ms, solved, scalars = gathered_sums(xs, inv_ref)
    rho = scalars[:, LANE_ZZ:LANE_ZZ + 1]
    alpha = rho / scalars[:, LANE_DU:LANE_DU + 1]
    squared = scalars[:, LANE_FF:LANE_FF + 1] - jnp.sum(ms * solved, axis=1, keepdims=True)
    rho_new = jnp.maximum(alpha * alpha * squared - rho, 0.0)
    beta = rho_new / rho
    for b in range(NP // BLK):
        y_out[b] = y_ref[b] - alpha * solved[:, b * BLK:(b + 1) * BLK]
    vectors = []
    for k in range(4):
        resid = r_ref[k] - alpha * xs[k][:, 0:M]
        direction = resid - expand(y_out, me_ref, w_ref, modes_ref, k) + beta * d_ref[k]
        vectors.append(direction)
        if k == 0:
            r_out[...] = resid
            d_out[...] = direction
    lam_out[...] = lam_ref[...] + alpha * d_ref[0]
    rho_out[...] = jnp.broadcast_to(rho_new, (NRHS, 128))
    apply_panel(me_ref, w_ref, modes_ref, vectors, panel_ref, pay_ref, None)


def last_kernel(me_ref, w_ref, img_ref, x0, x1, x2, x3, inv_ref, y_ref, r_ref, d_ref, lam_ref, rho_ref, modes_ref,
                lam_out, z_out, y_out):
    xs = (x0, x1, x2, x3)
    _, solved, scalars = gathered_sums(xs, inv_ref, 0)
    alpha = rho_ref[:, 0:1] / scalars[:, LANE_DU:LANE_DU + 1]
    for b in range(NP // BLK):
        y_out[b] = y_ref[b] - alpha * solved[:, b * BLK:(b + 1) * BLK]
    resid = r_ref[...] - alpha * img_ref[...]
    lam_out[...] = lam_ref[...] + alpha * d_ref[...]
    z_out[...] = resid - expand(y_out, me_ref, w_ref, modes_ref, 0)


def prepare_kernel(own_ref, partner_ref, count_ref, modes_ref, gap_ref, loads_ref, out_ref, side_ref, tile_ref):
    own = own_ref[0]
    partner = partner_ref[0, 0]
    count = count_ref[own]
    weight = jnp.where(partner >= 0, jnp.where(own < partner, 1.0, -1.0), 0.0).astype(F32)
    out_ref[0:MODES, 0:M] = modes_ref[0, 0]
    out_ref[MODES:PAD, 0:M] = jnp.zeros((PAD - MODES, M), F32)
    out_ref[:, M:2 * M] = gap_ref[0, 0]
    side_ref[...] = jnp.zeros((128, M), F32)
    side_ref[0:8, :] = out_ref[:, 0:M]
    side_ref[16:24, :] = out_ref[:, M:2 * M]
    tile_ref[...] = jnp.zeros((PAD, 128), F32)
    tile_ref[0:MODES, 8:16] = loads_ref[0]
    products = lax.dot_general(
        out_ref[:, 0:M], side_ref[...], (((1,), (1,)), ((), ())), precision=HIGHEST, preferred_element_type=F32
    )
    lane = lanes((PAD, 128))
    active = rows_of((PAD, 128)) < count
    tile = jnp.where(lane < 8, products, jnp.where(active, tile_ref[...] + weight * products, 0.0))
    tile = jnp.where(lane == 6, partner.astype(F32), tile)
    out_ref[:, 2 * M:] = jnp.where(lane == 7, count.astype(F32), tile)


def shift(value, axis, step):
    size = lax.axis_size(axis)
    return lax.ppermute(value, axis, [(i, (i + step) % size) for i in range(size)])


def front_gather(value):
    return [value] + [shift(value, "x", k) for k in range(1, 4)]


def to_line(value):
    return lax.all_to_all(jnp.broadcast_to(value[None], (8,) + value.shape), "z", 0, 0, tiled=True)


def sub_gather(value):
    width = value.shape[-1]
    along_z = to_line(value)
    own = jnp.concatenate([along_z] + [shift(along_z, "y", k) for k in range(1, 4)], axis=0)
    other = shift(own, "c", 1)
    return own.reshape(HALF, NRHS, width), other.reshape(HALF, NRHS, width)


def sds(*shape):
    return jax.ShapeDtypeStruct(shape, F32)


def coarse_call(sub_counts, me, weights, rows, modes_all, panels):
    return pl.pallas_call(
        coarse_kernel,
        out_shape=(
            jax.ShapeDtypeStruct((3, NP, NP), BF16), sds(4, NRHS, 128), sds(NRHS, M), sds(NRHS, W_U)
        ),
        in_specs=[SMEM, SMEM, SMEM, VMEM, VMEM, ANY],
        out_specs=(VMEM,) * 4,
        scratch_shapes=[
            pltpu.VMEM((NP, NP), F32),
            pltpu.VMEM((BLK, BLK), F32),
            pltpu.VMEM((4, NRHS, 128), F32),
            pltpu.VMEM((1, M, 4 * M), BF16),
            pltpu.SemaphoreType.DMA,
        ],
        compiler_params=pltpu.CompilerParams(vmem_limit_bytes=50 * 1024 * 1024),
        name="coarse",
    )(sub_counts, me, weights, rows, modes_all, panels)


def shards(panels, gap, modes, mode_loads, partners, counts):
    z_me, y_me, c_me, x_me = (lax.axis_index(a) for a in ("z", "y", "c", "x"))
    own = (z_me * 4 + y_me) * 2 + c_me
    prepared = pl.pallas_call(
        prepare_kernel,
        out_shape=sds(PAD, 2 * M + 128),
        in_specs=[SMEM, SMEM, SMEM, VMEM, VMEM, VMEM],
        out_specs=VMEM,
        scratch_shapes=[pltpu.VMEM((128, M), F32), pltpu.VMEM((PAD, 128), F32)],
        compiler_params=PARAMS,
        name="prepare",
    )(own[None].astype(jnp.int32), partners, counts, modes, gap, mode_loads)
    gathered = front_gather(prepared)
    modes_all = jnp.stack([g[:, 0:M] for g in gathered])
    gap_all = jnp.stack([g[:, M:2 * M] for g in gathered])
    tiles = [g[:, 2 * M:] for g in gathered]
    packed = jnp.concatenate(
        [t[:, 0:8] for t in tiles]
        + [tiles[0][:, 8:16], tiles[0][:, 16:24] + tiles[1][:, 16:24] + tiles[2][:, 16:24] + tiles[3][:, 16:24]]
        + [jnp.zeros((PAD, 80), F32)],
        axis=1,
    )
    mates = jnp.stack([t[0, 6] for t in tiles]).astype(jnp.int32)
    weights = jnp.where(own < mates, 1.0, -1.0).astype(F32) * (mates >= 0).astype(F32)

    def place_of(sub):
        return jnp.where(sub >= 0, (sub & 7) * 8 + (sub >> 3), -1)

    me = jnp.concatenate(
        [jnp.stack([c_me, y_me, place_of(own), x_me]), jnp.maximum(place_of(mates), 0)]
    ).astype(jnp.int32)
    along_z = to_line(packed)
    spread = jnp.broadcast_to(along_z[None], (8,) + along_z.shape)
    coarse_rows = lax.all_to_all(spread, ("y", "c"), 0, 0, tiled=True).reshape(SUBS, PAD, 128)
    heads = coarse_rows[:, 0, 6:8].astype(jnp.int32)
    mate_places = place_of(heads[:, 0])
    sub_counts = heads[:, 1]

    inverse, y_gap, lam, payload = coarse_call(
        sub_counts, me, weights, coarse_rows.reshape(NP, 128), modes_all, panels
    )

    def exchange_all(payload):
        return pl.pallas_call(
            mate_kernel,
            out_shape=sds(NRHS, W_X),
            in_specs=[SMEM] * 4 + [ANY, ANY],
            out_specs=VMEM,
            scratch_shapes=[pltpu.VMEM((SUBS, NRHS, W_U), F32), pltpu.SemaphoreType.DMA((2,))],
            compiler_params=PARAMS,
            name="mate",
        )(mate_places, sub_counts, me, weights, *sub_gather(payload))

    def exchange(payload, name):
        chosen = pl.pallas_call(
            choose_kernel,
            out_shape=sds(8, NRHS, W_U),
            in_specs=[SMEM, SMEM, VMEM],
            out_specs=VMEM,
            compiler_params=PARAMS,
            name="choose_" + name,
        )(mate_places, me, to_line(payload))
        got = lax.all_to_all(chosen, ("y", "c"), 0, 0, tiled=True)
        return pl.pallas_call(
            match_kernel,
            out_shape=(sds(NRHS, M), sds(NRHS, NP + 128)),
            in_specs=[SMEM] * 4 + [VMEM, VMEM],
            out_specs=(VMEM, VMEM),
            scratch_shapes=[pltpu.VMEM((4, NRHS, 128), F32)],
            compiler_params=PARAMS,
            name="match_" + name,
        )(mate_places, sub_counts, me, weights, payload, got)

    xs = front_gather(jnp.concatenate(exchange(payload, "begin"), axis=1))
    resid, direction, y_resid, payload = pl.pallas_call(
        first_kernel,
        out_shape=(sds(4, NRHS, M), sds(4, NRHS, M), sds(4, NRHS, 128), sds(NRHS, W_U)),
        in_specs=[SMEM, SMEM] + [VMEM] * 9,
        out_specs=(VMEM,) * 4,
        compiler_params=PARAMS,
        name="first",
    )(me, weights, *xs, inverse, y_gap, gap_all, modes_all, panels)

    xs = front_gather(exchange_all(payload))
    resid, direction, y_resid, lam, rho, payload = pl.pallas_call(
        second_kernel,
        out_shape=(sds(NRHS, M), sds(NRHS, M), sds(4, NRHS, 128), sds(NRHS, M), sds(NRHS, 128), sds(NRHS, W_U)),
        in_specs=[SMEM, SMEM] + [VMEM] * 11,
        out_specs=(VMEM,) * 6,
        compiler_params=PARAMS,
        name="second",
    )(me, weights, *xs, inverse, y_resid, resid, direction, lam, modes_all, panels)

    image, sums = exchange(payload, "second")
    xs = front_gather(sums)
    lam, projected, _ = pl.pallas_call(
        last_kernel,
        out_shape=(sds(NRHS, M), sds(NRHS, M), sds(4, NRHS, 128)),
        in_specs=[SMEM, SMEM] + [VMEM] * 12,
        out_specs=(VMEM,) * 3,
        compiler_params=PARAMS,
        name="last",
    )(me, weights, image, *xs, inverse, y_resid, resid, direction, lam, rho, modes_all)
    return (lam[None, None], projected[None, None])


def solution(mesh):
    fine = Mesh(mesh.devices.reshape(8, 4, 2, 4), ("z", "y", "c", "x"))
    sub = ("z", "y", "c")
    in_specs = (
        P(sub, "x", None),
        P(sub, "x", None, None),
        P(sub, "x", None, None),
        P(sub, None, None),
        P(sub, "x"),
        P(),
    )
    out_specs = (P(sub, "x", None, None), P(sub, "x", None, None))
    return jax.shard_map(shards, mesh=fine, in_specs=in_specs, out_specs=out_specs, check_vma=False)
```

```python
import functools

import jax
import jax.numpy as jnp
from jax import lax
from jax.experimental import pallas as pl
from jax.experimental.pallas import tpu as pltpu
from jax.sharding import Mesh, PartitionSpec as P

MODES = 6
NRHS = 8
M = 768
SUBS = 64
PAD = 8
NP = SUBS * PAD
BLK = 128
HALF = SUBS // 2
HIGHEST = lax.Precision.HIGHEST
F32 = jnp.float32
BF16 = jnp.bfloat16

LANE_DU, LANE_ZZ, LANE_FF = 6, 7, 8
W_U = M + 128
W_X = M + NP + 128

SMEM = pl.BlockSpec(memory_space=pltpu.SMEM)
VMEM = pl.BlockSpec(memory_space=pltpu.VMEM)
ANY = pl.BlockSpec(memory_space=pl.ANY)
PARAMS = pltpu.CompilerParams(vmem_limit_bytes=16 * 1024 * 1024)


def lanes(shape):
    return lax.broadcasted_iota(jnp.int32, shape, len(shape) - 1)


def rows_of(shape):
    return lax.broadcasted_iota(jnp.int32, shape, 0)


def dot_high(a, b):
    return jnp.dot(a, b, precision=HIGHEST, preferred_element_type=F32)


def split(x):
    high = x.astype(BF16).astype(F32)
    rest = x - high
    middle = rest.astype(BF16).astype(F32)
    return high, middle, rest - middle


def dot_six(a, b):
    ah, am, al = (p.astype(BF16) for p in split(a))
    bh, bm, bl = (p.astype(BF16) for p in split(b))
    left = jnp.concatenate([ah, am, ah, am, ah, al], axis=1)
    right = jnp.concatenate([bh, bh, bm, bm, bl, bh], axis=0)
    return jnp.dot(left, right, preferred_element_type=F32)


def dot_pieces(a, pieces_ref):
    stacked = jnp.concatenate(split(a), axis=0)
    rows = a.shape[0]
    part = jnp.dot(stacked.astype(BF16), pieces_ref[0], preferred_element_type=F32)
    total = part[0:rows] + part[rows:2 * rows] + part[2 * rows:3 * rows]
    part = jnp.dot(stacked[0:2 * rows].astype(BF16), pieces_ref[1], preferred_element_type=F32)
    total = total + (part[0:rows] + part[rows:2 * rows])
    return total + jnp.dot(stacked[0:rows].astype(BF16), pieces_ref[2], preferred_element_type=F32)


def coarse_kernel(cnt_ref, me_ref, w_ref, own_ref, oth_ref, modes_ref, panel_ref,
                  inv_ref, yg_ref, lam_ref, pay_ref, g_ref, a_ref, d_ref, y0_ref, held_ref, sem):
    copy = pltpu.make_async_copy(panel_ref, held_ref, sem)
    copy.start()
    core = me_ref[0]
    for y in range(4):
        for z in range(8):
            g_ref[2 * y * 8 + core * 8 + z] = own_ref[z * 4 + y]
            g_ref[2 * y * 8 + (1 - core) * 8 + z] = oth_ref[z * 4 + y]
    flipped = g_ref[...].reshape(NP, 128).T
    column = lanes((PAD, NP))
    row = rows_of((PAD, NP))
    column_sub = lax.shift_right_logical(column, 3)
    column_active = lax.bitwise_and(column, 7) < flipped[7:8, :].astype(jnp.int32)
    grams, places = [], []
    for k in range(4):
        mate = jnp.broadcast_to(flipped[8 * k + 6:8 * k + 7, :].astype(jnp.int32), (PAD, NP))
        places.append(lax.bitwise_and(mate, 7) * 8 + lax.shift_right_logical(mate, 3))
        keep = (row < MODES) & column_active & (mate >= 0)
        grams.append(jnp.where(keep, flipped[8 * k:8 * k + 8, :], 0.0))
    whole = grams[0] + grams[1] + grams[2] + grams[3]
    for t in range(SUBS):
        total = jnp.where(column_sub == t, whole, 0.0)
        for k in range(4):
            total = total - jnp.where(places[k] == t, grams[k], 0.0)
        identity = jnp.where(column == PAD * t + row, 1.0, 0.0)
        a_ref[PAD * t:PAD * t + PAD, :] = jnp.where(row < cnt_ref[t], total, identity)
    lane = lanes((BLK, BLK))

    tile_lane = lanes((PAD, BLK))
    tile_row = rows_of((PAD, BLK))

    def sweep(i, pivots):
        p = PAD * i
        rows = d_ref[p:p + PAD, :]
        columns = [jnp.broadcast_to(rows[:, p + b:p + b + 1], (PAD, BLK)) for b in range(pivots)]
        s = [[None] * pivots for _ in range(pivots)]
        for b in range(pivots):
            for a in range(b + 1):
                s[a][b] = jnp.broadcast_to(columns[b][a:a + 1, :], (PAD, BLK))
        for v in range(pivots):
            over = 1.0 / s[v][v]
            line = [s[min(v, b)][max(v, b)] for b in range(pivots)]
            scaled = [x * over for x in line]
            for a in range(pivots):
                for b in range(a, pivots):
                    if a != v and b != v:
                        s[a][b] = s[a][b] - line[a] * scaled[b]
            for b in range(pivots):
                if b != v:
                    s[min(v, b)][max(v, b)] = scaled[b]
            s[v][v] = -over
        new_rows = jnp.zeros((PAD, BLK), F32)
        tails = []
        for b in range(pivots):
            column = jnp.zeros((PAD, BLK), F32)
            for a in range(pivots):
                column = jnp.where(tile_row == a, s[min(a, b)][max(a, b)], column)
            new_rows = new_rows - column * rows[b:b + 1, :]
            tails.append(column)
        for b in range(pivots):
            new_rows = jnp.where(tile_lane == p + b, tails[b], new_rows)
        mat = d_ref[...]
        new = jnp.where((lane >= p) & (lane < p + pivots), 0.0, mat)
        for b in range(pivots):
            new = new - mat[:, p + b:p + b + 1] * new_rows[b:b + 1, :]
        d_ref[...] = new
        d_ref[p:p + PAD, :] = jnp.where(tile_row < pivots, new_rows, rows)

    for b in range(NP // BLK):
        lo, hi = b * BLK, (b + 1) * BLK
        d_ref[...] = a_ref[lo:hi, lo:hi]

        for i in range(BLK // PAD):
            count = cnt_ref[b * (BLK // PAD) + i]
            for low, high in ((1, 3), (4, 6)):
                @pl.when((count >= low) & (count <= high))
                def _(i=i, high=high):
                    sweep(i, high)

        small = -d_ref[...]
        tall = a_ref[:, lo:hi]
        wide = dot_six(small, a_ref[lo:hi, :])
        a_ref[...] = a_ref[...] - dot_six(tall, wide)
        a_ref[:, lo:hi] = dot_six(tall, small)
        a_ref[lo:hi, :] = wide
        a_ref[lo:hi, lo:hi] = -small
    pieces = split(-a_ref[...])
    for n in range(3):
        inv_ref[n] = pieces[n].astype(BF16)
    y = dot_pieces(flipped[32:48, :], inv_ref)
    for b in range(NP // BLK):
        y0_ref[b] = y[0:8, b * BLK:(b + 1) * BLK]
        yg_ref[b] = y[8:16, b * BLK:(b + 1) * BLK]
    vectors = [expand(y0_ref, me_ref, w_ref, modes_ref, k) for k in range(4)]
    lam_ref[...] = vectors[0]
    copy.wait()
    apply_panel(me_ref, w_ref, modes_ref, vectors, held_ref, pay_ref, None)


def mate_kernel(mate_ref, cnt_ref, me_ref, w_ref, own_ref, oth_ref, out_ref, g_ref, sems):
    first = pltpu.make_async_copy(own_ref, g_ref.at[0:HALF], sems.at[0])
    second = pltpu.make_async_copy(oth_ref, g_ref.at[HALF:SUBS], sems.at[1])
    first.start()
    second.start()
    first.wait()
    second.wait()
    core, y_me = me_ref[0], me_ref[1]

    def held(place):
        group = lax.shift_right_logical(place, 3)
        apart = lax.bitwise_and(y_me - lax.shift_right_logical(group, 1), 3)
        return lax.bitwise_xor(lax.bitwise_and(group, 1), core) * HALF + apart * 8 + lax.bitwise_and(place, 7)

    mine = held(me_ref[2])
    theirs = held(me_ref[4])
    out_ref[:, 0:M] = w_ref[0] * (g_ref[mine][:, 0:M] - g_ref[theirs][:, 0:M])
    lane = lanes((NRHS, 128))
    sums = [jnp.zeros((NRHS, 128), F32) for _ in range(NP // BLK)]
    scalars = jnp.zeros((NRHS, 128), F32)
    norm = jnp.zeros((NRHS, M), F32)
    for p in range(SUBS):
        mate = mate_ref[p]
        used = (mate >= 0).astype(F32)
        here = held(jnp.int32(p))
        at = held(jnp.maximum(mate, 0))
        tile = g_ref[here, :, M:W_U]
        scalars = scalars + tile
        limit = jnp.where(mate >= 0, cnt_ref[p], 0)
        piece = jnp.where(lane < limit, tile - g_ref[at, :, M:W_U], 0.0)
        if p % 16:
            piece = pltpu.roll(piece, 8 * (p % 16), 1)
        sums[p // 16] = sums[p // 16] + piece
        gone = g_ref[here, :, 0:M] - g_ref[at, :, 0:M]
        norm = norm + used * (gone * gone)
    for b in range(NP // BLK):
        out_ref[:, M + b * BLK:M + (b + 1) * BLK] = sums[b]
    scalars = jnp.where(lane == LANE_FF, 0.5 * jnp.sum(norm, axis=1, keepdims=True), scalars)
    out_ref[:, M + NP:W_X] = scalars


def choose_kernel(mate_ref, me_ref, z_ref, out_ref):
    lane = lanes((NRHS, 128))
    tail = jnp.where(lane < 8, z_ref[0, :, M:W_U], 0.0)
    for z in range(1, 8):
        tail = tail + pltpu.roll(jnp.where(lane < 8, z_ref[z, :, M:W_U], 0.0), 8 * z, 1)
    for group in range(8):
        mate = jnp.maximum(mate_ref[group * 8 + lax.bitwise_and(me_ref[2], 7)], 0)
        out_ref[group, :, 0:M] = z_ref[lax.bitwise_and(mate, 7), :, 0:M]
        out_ref[group, :, M:W_U] = tail


def match_kernel(mate_ref, cnt_ref, me_ref, w_ref, own_ref, got_ref, img_ref, sum_ref, q_ref):
    theirs = lax.shift_right_logical(me_ref[4], 3)
    img_ref[...] = w_ref[0] * (own_ref[:, 0:M] - got_ref[theirs][:, 0:M])
    lane = lanes((NRHS, 128))
    scalars = jnp.zeros((NRHS, 128), F32)
    for b in range(NP // BLK):
        both = got_ref[2 * b, :, M:W_U] + pltpu.roll(got_ref[2 * b + 1, :, M:W_U], 64, 1)
        q_ref[b] = both
        scalars = scalars + both
    for step in (8, 16, 32, 64):
        scalars = scalars + pltpu.roll(scalars, step, 1)
    for b in range(NP // BLK):
        total = jnp.zeros((NRHS, 128), F32)
        here = q_ref[b]
        for i in range(16):
            p = b * 16 + i
            mate = mate_ref[p]
            at = jnp.maximum(mate, 0)
            step = lax.bitwise_and(8 * (i - at), 127)
            there = pltpu.roll(q_ref[lax.shift_right_logical(at, 4)], step, 1)
            limit = 8 * i + jnp.where(mate >= 0, cnt_ref[p], 0)
            total = jnp.where((lane >= 8 * i) & (lane < limit), here - there, total)
        sum_ref[:, b * BLK:(b + 1) * BLK] = total
    sum_ref[:, NP:NP + 128] = scalars


def y_at(y_ref, place):
    tile = y_ref[lax.div(place, 16)]
    return pltpu.roll(tile, lax.rem(128 - 8 * lax.rem(place, 16), 128), 1)


def expand(y_ref, me_ref, w_ref, modes_ref, k):
    coeff = y_at(y_ref, me_ref[2]) - y_at(y_ref, me_ref[4 + k])
    total = coeff[:, 0:1] * modes_ref[k, 0:1, :]
    for m in range(1, MODES):
        total = total + coeff[:, m:m + 1] * modes_ref[k, m:m + 1, :]
    return w_ref[k] * total


def apply_panel(me_ref, w_ref, modes_ref, vectors, panel_ref, pay_ref, square):
    total = None
    for k in range(4):
        load = (w_ref[k] * vectors[k]).astype(BF16)
        at = pl.multiple_of(lax.bitwise_and(me_ref[3] - k, 3) * M, M)
        slot = panel_ref[0, :, pl.ds(at, M)]
        part = lax.dot_general(load, slot, (((1,), (1,)), ((), ())), preferred_element_type=F32)
        total = part if total is None else total + part
    lane = lanes((NRHS, 128))
    tail = jnp.zeros((NRHS, 128), F32)
    for m in range(MODES):
        tail = jnp.where(lane == m, jnp.sum(total * modes_ref[0, m:m + 1, :], axis=1, keepdims=True), tail)
    dots = jnp.sum(w_ref[0] * vectors[0] * total, axis=1, keepdims=True)
    tail = jnp.where(lane == LANE_DU, dots, tail)
    if square is not None:
        tail = jnp.where(lane == LANE_ZZ, 0.5 * jnp.sum(square * square, axis=1, keepdims=True), tail)
    pay_ref[:, 0:M] = total
    pay_ref[:, M:W_U] = tail


def gathered_sums(x_refs, inv_ref, at=M):
    ms = x_refs[0][:, at:at + NP]
    scalars = x_refs[0][:, at + NP:at + NP + 128]
    for ref in x_refs[1:]:
        ms = ms + ref[:, at:at + NP]
        scalars = scalars + ref[:, at + NP:at + NP + 128]
    return ms, dot_pieces(ms, inv_ref), scalars


def first_kernel(me_ref, w_ref, x0, x1, x2, x3, inv_ref, yg_ref, gap_ref, modes_ref, panel_ref,
                 r_ref, z_ref, y_ref, pay_ref):
    xs = (x0, x1, x2, x3)
    _, solved, _ = gathered_sums(xs, inv_ref)
    for b in range(NP // BLK):
        y_ref[b] = yg_ref[b] - solved[:, b * BLK:(b + 1) * BLK]
    vectors = []
    for k in range(4):
        resid = w_ref[k] * w_ref[k] * gap_ref[k] - xs[k][:, 0:M]
        r_ref[k] = resid
        z = resid - expand(y_ref, me_ref, w_ref, modes_ref, k)
        z_ref[k] = z
        vectors.append(z)
    apply_panel(me_ref, w_ref, modes_ref, vectors, panel_ref, pay_ref, vectors[0])


def second_kernel(me_ref, w_ref, x0, x1, x2, x3, inv_ref, y_ref, r_ref, d_ref, lam_ref, modes_ref, panel_ref,
                  r_out, d_out, y_out, lam_out, rho_out, pay_ref):
    xs = (x0, x1, x2, x3)
    ms, solved, scalars = gathered_sums(xs, inv_ref)
    rho = scalars[:, LANE_ZZ:LANE_ZZ + 1]
    alpha = rho / scalars[:, LANE_DU:LANE_DU + 1]
    squared = scalars[:, LANE_FF:LANE_FF + 1] - jnp.sum(ms * solved, axis=1, keepdims=True)
    rho_new = jnp.maximum(alpha * alpha * squared - rho, 0.0)
    beta = rho_new / rho
    for b in range(NP // BLK):
        y_out[b] = y_ref[b] - alpha * solved[:, b * BLK:(b + 1) * BLK]
    vectors = []
    for k in range(4):
        resid = r_ref[k] - alpha * xs[k][:, 0:M]
        direction = resid - expand(y_out, me_ref, w_ref, modes_ref, k) + beta * d_ref[k]
        vectors.append(direction)
        if k == 0:
            r_out[...] = resid
            d_out[...] = direction
    lam_out[...] = lam_ref[...] + alpha * d_ref[0]
    rho_out[...] = jnp.broadcast_to(rho_new, (NRHS, 128))
    apply_panel(me_ref, w_ref, modes_ref, vectors, panel_ref, pay_ref, None)


def last_kernel(me_ref, w_ref, img_ref, x0, x1, x2, x3, inv_ref, y_ref, r_ref, d_ref, lam_ref, rho_ref, modes_ref,
                lam_out, z_out, y_out):
    xs = (x0, x1, x2, x3)
    _, solved, scalars = gathered_sums(xs, inv_ref, 0)
    alpha = rho_ref[:, 0:1] / scalars[:, LANE_DU:LANE_DU + 1]
    for b in range(NP // BLK):
        y_out[b] = y_ref[b] - alpha * solved[:, b * BLK:(b + 1) * BLK]
    resid = r_ref[...] - alpha * img_ref[...]
    lam_out[...] = lam_ref[...] + alpha * d_ref[...]
    z_out[...] = resid - expand(y_out, me_ref, w_ref, modes_ref, 0)


def prepare_kernel(own_ref, partner_ref, count_ref, modes_ref, gap_ref, loads_ref, out_ref, side_ref, tile_ref):
    own = own_ref[0]
    partner = partner_ref[0, 0]
    count = count_ref[own]
    weight = jnp.where(partner >= 0, jnp.where(own < partner, 1.0, -1.0), 0.0).astype(F32)
    out_ref[0:MODES, 0:M] = modes_ref[0, 0]
    out_ref[MODES:PAD, 0:M] = jnp.zeros((PAD - MODES, M), F32)
    out_ref[:, M:2 * M] = gap_ref[0, 0]
    side_ref[...] = jnp.zeros((128, M), F32)
    side_ref[0:8, :] = out_ref[:, 0:M]
    side_ref[16:24, :] = out_ref[:, M:2 * M]
    tile_ref[...] = jnp.zeros((PAD, 128), F32)
    tile_ref[0:MODES, 8:16] = loads_ref[0]
    products = lax.dot_general(
        out_ref[:, 0:M], side_ref[...], (((1,), (1,)), ((), ())), precision=HIGHEST, preferred_element_type=F32
    )
    lane = lanes((PAD, 128))
    active = rows_of((PAD, 128)) < count
    tile = jnp.where(lane < 8, products, jnp.where(active, tile_ref[...] + weight * products, 0.0))
    tile = jnp.where(lane == 6, partner.astype(F32), tile)
    out_ref[:, 2 * M:] = jnp.where(lane == 7, count.astype(F32), tile)


def shift(value, axis, step):
    size = lax.axis_size(axis)
    return lax.ppermute(value, axis, [(i, (i + step) % size) for i in range(size)])


def front_gather(value):
    return [value] + [shift(value, "x", k) for k in range(1, 4)]


def to_line(value):
    return lax.all_to_all(jnp.broadcast_to(value[None], (8,) + value.shape), "z", 0, 0, tiled=True)


def sub_gather(value):
    width = value.shape[-1]
    along_z = to_line(value)
    own = jnp.concatenate([along_z] + [shift(along_z, "y", k) for k in range(1, 4)], axis=0)
    other = shift(own, "c", 1)
    return own.reshape(HALF, NRHS, width), other.reshape(HALF, NRHS, width)


def sds(*shape):
    return jax.ShapeDtypeStruct(shape, F32)


def coarse_call(sub_counts, me, weights, near, far, modes_all, panels):
    return pl.pallas_call(
        coarse_kernel,
        out_shape=(
            jax.ShapeDtypeStruct((3, NP, NP), BF16), sds(4, NRHS, 128), sds(NRHS, M), sds(NRHS, W_U)
        ),
        in_specs=[SMEM, SMEM, SMEM, VMEM, VMEM, VMEM, ANY],
        out_specs=(VMEM,) * 4,
        scratch_shapes=[
            pltpu.VMEM((SUBS, PAD, 128), F32),
            pltpu.VMEM((NP, NP), F32),
            pltpu.VMEM((BLK, BLK), F32),
            pltpu.VMEM((4, NRHS, 128), F32),
            pltpu.VMEM((1, M, 4 * M), BF16),
            pltpu.SemaphoreType.DMA,
        ],
        compiler_params=pltpu.CompilerParams(vmem_limit_bytes=50 * 1024 * 1024),
        name="coarse",
    )(sub_counts, me, weights, near, far, modes_all, panels)


def shards(panels, gap, modes, mode_loads, partners, counts):
    z_me, y_me, c_me, x_me = (lax.axis_index(a) for a in ("z", "y", "c", "x"))
    own = (z_me * 4 + y_me) * 2 + c_me
    prepared = pl.pallas_call(
        prepare_kernel,
        out_shape=sds(PAD, 2 * M + 128),
        in_specs=[SMEM, SMEM, SMEM, VMEM, VMEM, VMEM],
        out_specs=VMEM,
        scratch_shapes=[pltpu.VMEM((128, M), F32), pltpu.VMEM((PAD, 128), F32)],
        compiler_params=PARAMS,
        name="prepare",
    )(own[None].astype(jnp.int32), partners, counts, modes, gap, mode_loads)
    gathered = front_gather(prepared)
    modes_all = jnp.stack([g[:, 0:M] for g in gathered])
    gap_all = jnp.stack([g[:, M:2 * M] for g in gathered])
    tiles = [g[:, 2 * M:] for g in gathered]
    packed = jnp.concatenate(
        [t[:, 0:8] for t in tiles]
        + [tiles[0][:, 8:16], tiles[0][:, 16:24] + tiles[1][:, 16:24] + tiles[2][:, 16:24] + tiles[3][:, 16:24]]
        + [jnp.zeros((PAD, 80), F32)],
        axis=1,
    )
    mates = jnp.stack([t[0, 6] for t in tiles]).astype(jnp.int32)
    weights = jnp.where(own < mates, 1.0, -1.0).astype(F32) * (mates >= 0).astype(F32)

    def place_of(sub):
        return jnp.where(sub >= 0, (sub & 7) * 8 + (sub >> 3), -1)

    me = jnp.concatenate(
        [jnp.stack([c_me, y_me, place_of(own), x_me]), jnp.maximum(place_of(mates), 0)]
    ).astype(jnp.int32)
    spread = jnp.broadcast_to(packed[None], (HALF, PAD, 128))
    near = lax.all_to_all(spread, ("z", "y"), 0, 0, tiled=True)
    far = shift(near, "c", 1)
    heads = jnp.stack([near[:, 0, 6], far[:, 0, 6]])
    heads = jnp.where(c_me == 0, heads, heads[::-1]).astype(jnp.int32).reshape(2, 8, 4)
    mate_places = place_of(heads.transpose(2, 0, 1).reshape(SUBS))
    sub_counts = counts.reshape(8, 8).T.reshape(SUBS)

    inverse, y_gap, lam, payload = coarse_call(
        sub_counts, me, weights, near, far, modes_all, panels
    )

    def exchange_all(payload):
        return pl.pallas_call(
            mate_kernel,
            out_shape=sds(NRHS, W_X),
            in_specs=[SMEM] * 4 + [ANY, ANY],
            out_specs=VMEM,
            scratch_shapes=[pltpu.VMEM((SUBS, NRHS, W_U), F32), pltpu.SemaphoreType.DMA((2,))],
            compiler_params=PARAMS,
            name="mate",
        )(mate_places, sub_counts, me, weights, *sub_gather(payload))

    def exchange(payload, name):
        chosen = pl.pallas_call(
            choose_kernel,
            out_shape=sds(8, NRHS, W_U),
            in_specs=[SMEM, SMEM, VMEM],
            out_specs=VMEM,
            compiler_params=PARAMS,
            name="choose_" + name,
        )(mate_places, me, to_line(payload))
        got = lax.all_to_all(chosen, ("y", "c"), 0, 0, tiled=True)
        return pl.pallas_call(
            match_kernel,
            out_shape=(sds(NRHS, M), sds(NRHS, NP + 128)),
            in_specs=[SMEM] * 4 + [VMEM, VMEM],
            out_specs=(VMEM, VMEM),
            scratch_shapes=[pltpu.VMEM((4, NRHS, 128), F32)],
            compiler_params=PARAMS,
            name="match_" + name,
        )(mate_places, sub_counts, me, weights, payload, got)

    xs = front_gather(jnp.concatenate(exchange(payload, "begin"), axis=1))
    resid, direction, y_resid, payload = pl.pallas_call(
        first_kernel,
        out_shape=(sds(4, NRHS, M), sds(4, NRHS, M), sds(4, NRHS, 128), sds(NRHS, W_U)),
        in_specs=[SMEM, SMEM] + [VMEM] * 9,
        out_specs=(VMEM,) * 4,
        compiler_params=PARAMS,
        name="first",
    )(me, weights, *xs, inverse, y_gap, gap_all, modes_all, panels)

    xs = front_gather(exchange_all(payload))
    resid, direction, y_resid, lam, rho, payload = pl.pallas_call(
        second_kernel,
        out_shape=(sds(NRHS, M), sds(NRHS, M), sds(4, NRHS, 128), sds(NRHS, M), sds(NRHS, 128), sds(NRHS, W_U)),
        in_specs=[SMEM, SMEM] + [VMEM] * 11,
        out_specs=(VMEM,) * 6,
        compiler_params=PARAMS,
        name="second",
    )(me, weights, *xs, inverse, y_resid, resid, direction, lam, modes_all, panels)

    image, sums = exchange(payload, "second")
    xs = front_gather(sums)
    lam, projected, _ = pl.pallas_call(
        last_kernel,
        out_shape=(sds(NRHS, M), sds(NRHS, M), sds(4, NRHS, 128)),
        in_specs=[SMEM, SMEM] + [VMEM] * 12,
        out_specs=(VMEM,) * 3,
        compiler_params=PARAMS,
        name="last",
    )(me, weights, image, *xs, inverse, y_resid, resid, direction, lam, rho, modes_all)
    return (lam[None, None], projected[None, None])


def solution(mesh):
    fine = Mesh(mesh.devices.reshape(8, 4, 2, 4), ("z", "y", "c", "x"))
    sub = ("z", "y", "c")
    in_specs = (
        P(sub, "x", None),
        P(sub, "x", None, None),
        P(sub, "x", None, None),
        P(sub, None, None),
        P(sub, "x"),
        P(),
    )
    out_specs = (P(sub, "x", None, None), P(sub, "x", None, None))
    return jax.shard_map(shards, mesh=fine, in_specs=in_specs, out_specs=out_specs, check_vma=False)
```

```python
import functools

import jax
import jax.numpy as jnp
from jax import lax
from jax.experimental import pallas as pl
from jax.experimental.pallas import tpu as pltpu
from jax.sharding import Mesh, PartitionSpec as P

MODES = 6
NRHS = 8
M = 768
SUBS = 64
PAD = 8
NP = SUBS * PAD
BLK = 128
HALF = SUBS // 2
HIGHEST = lax.Precision.HIGHEST
F32 = jnp.float32
BF16 = jnp.bfloat16

LANE_DU, LANE_ZZ, LANE_FF = 6, 7, 8
W_U = M + 128
W_X = M + NP + 128

SMEM = pl.BlockSpec(memory_space=pltpu.SMEM)
VMEM = pl.BlockSpec(memory_space=pltpu.VMEM)
ANY = pl.BlockSpec(memory_space=pl.ANY)
PARAMS = pltpu.CompilerParams(vmem_limit_bytes=16 * 1024 * 1024)


def lanes(shape):
    return lax.broadcasted_iota(jnp.int32, shape, len(shape) - 1)


def rows_of(shape):
    return lax.broadcasted_iota(jnp.int32, shape, 0)


def dot_high(a, b):
    return jnp.dot(a, b, precision=HIGHEST, preferred_element_type=F32)


def split(x):
    high = x.astype(BF16).astype(F32)
    rest = x - high
    middle = rest.astype(BF16).astype(F32)
    return high, middle, rest - middle


def dot_six(a, b):
    ah, am, al = (p.astype(BF16) for p in split(a))
    bh, bm, bl = (p.astype(BF16) for p in split(b))
    left = jnp.concatenate([ah, am, ah, am, ah, al], axis=1)
    right = jnp.concatenate([bh, bh, bm, bm, bl, bh], axis=0)
    return jnp.dot(left, right, preferred_element_type=F32)


def dot_pieces(a, pieces_ref):
    stacked = jnp.concatenate(split(a), axis=0)
    rows = a.shape[0]
    part = jnp.dot(stacked.astype(BF16), pieces_ref[0], preferred_element_type=F32)
    total = part[0:rows] + part[rows:2 * rows] + part[2 * rows:3 * rows]
    part = jnp.dot(stacked[0:2 * rows].astype(BF16), pieces_ref[1], preferred_element_type=F32)
    total = total + (part[0:rows] + part[rows:2 * rows])
    return total + jnp.dot(stacked[0:rows].astype(BF16), pieces_ref[2], preferred_element_type=F32)


def coarse_kernel(cnt_ref, me_ref, w_ref, own_ref, oth_ref, modes_ref, panel_ref,
                  inv_ref, yg_ref, lam_ref, pay_ref, g_ref, a_ref, d_ref, y0_ref, held_ref, sem):
    copy = pltpu.make_async_copy(panel_ref, held_ref, sem)
    copy.start()
    core = me_ref[0]
    for y in range(4):
        for z in range(8):
            g_ref[2 * y * 8 + core * 8 + z] = own_ref[z * 4 + y]
            g_ref[2 * y * 8 + (1 - core) * 8 + z] = oth_ref[z * 4 + y]
    flipped = g_ref[...].reshape(NP, 128).T
    column = lanes((PAD, NP))
    row = rows_of((PAD, NP))
    column_sub = lax.shift_right_logical(column, 3)
    column_active = lax.bitwise_and(column, 7) < flipped[7:8, :].astype(jnp.int32)
    grams, places = [], []
    for k in range(4):
        mate = jnp.broadcast_to(flipped[8 * k + 6:8 * k + 7, :].astype(jnp.int32), (PAD, NP))
        places.append(lax.bitwise_and(mate, 7) * 8 + lax.shift_right_logical(mate, 3))
        keep = (row < MODES) & column_active & (mate >= 0)
        grams.append(jnp.where(keep, flipped[8 * k:8 * k + 8, :], 0.0))
    whole = grams[0] + grams[1] + grams[2] + grams[3]
    for t in range(SUBS):
        total = jnp.where(column_sub == t, whole, 0.0)
        for k in range(4):
            total = total - jnp.where(places[k] == t, grams[k], 0.0)
        identity = jnp.where(column == PAD * t + row, 1.0, 0.0)
        a_ref[PAD * t:PAD * t + PAD, :] = jnp.where(row < cnt_ref[t], total, identity)
    lane = lanes((BLK, BLK))

    tile_lane = lanes((PAD, BLK))
    tile_row = rows_of((PAD, BLK))

    def sweep(i, pivots):
        p = PAD * i
        rows = d_ref[p:p + PAD, :]
        columns = [jnp.broadcast_to(rows[:, p + b:p + b + 1], (PAD, BLK)) for b in range(pivots)]
        s = [[None] * pivots for _ in range(pivots)]
        for b in range(pivots):
            for a in range(b + 1):
                s[a][b] = jnp.broadcast_to(columns[b][a:a + 1, :], (PAD, BLK))
        for v in range(pivots):
            over = 1.0 / s[v][v]
            line = [s[min(v, b)][max(v, b)] for b in range(pivots)]
            scaled = [x * over for x in line]
            for a in range(pivots):
                for b in range(a, pivots):
                    if a != v and b != v:
                        s[a][b] = s[a][b] - line[a] * scaled[b]
            for b in range(pivots):
                if b != v:
                    s[min(v, b)][max(v, b)] = scaled[b]
            s[v][v] = -over
        new_rows = jnp.zeros((PAD, BLK), F32)
        tails = []
        for b in range(pivots):
            column = jnp.zeros((PAD, BLK), F32)
            for a in range(pivots):
                column = jnp.where(tile_row == a, s[min(a, b)][max(a, b)], column)
            new_rows = new_rows - column * rows[b:b + 1, :]
            tails.append(column)
        for b in range(pivots):
            new_rows = jnp.where(tile_lane == p + b, tails[b], new_rows)
        mat = d_ref[...]
        new = jnp.where((lane >= p) & (lane < p + pivots), 0.0, mat)
        for b in range(pivots):
            new = new - mat[:, p + b:p + b + 1] * new_rows[b:b + 1, :]
        d_ref[...] = new
        d_ref[p:p + PAD, :] = jnp.where(tile_row < pivots, new_rows, rows)

    for b in range(NP // BLK):
        lo, hi = b * BLK, (b + 1) * BLK
        d_ref[...] = a_ref[lo:hi, lo:hi]

        for i in range(BLK // PAD):
            count = cnt_ref[b * (BLK // PAD) + i]
            for low, high in ((1, 3), (4, 6)):
                @pl.when((count >= low) & (count <= high))
                def _(i=i, high=high):
                    sweep(i, high)

        small = -d_ref[...]
        tall = a_ref[:, lo:hi]
        wide = dot_six(small, a_ref[lo:hi, :])
        a_ref[...] = a_ref[...] - dot_six(tall, wide)
        a_ref[:, lo:hi] = dot_six(tall, small)
        a_ref[lo:hi, :] = wide
        a_ref[lo:hi, lo:hi] = -small
    pieces = split(-a_ref[...])
    for n in range(3):
        inv_ref[n] = pieces[n].astype(BF16)
    y = dot_pieces(flipped[32:48, :], inv_ref)
    for b in range(NP // BLK):
        y0_ref[b] = y[0:8, b * BLK:(b + 1) * BLK]
        yg_ref[b] = y[8:16, b * BLK:(b + 1) * BLK]
    vectors = [expand(y0_ref, me_ref, w_ref, modes_ref, k) for k in range(4)]
    lam_ref[...] = vectors[0]
    copy.wait()
    apply_panel(me_ref, w_ref, modes_ref, vectors, held_ref, pay_ref, None)


def mate_kernel(mate_ref, cnt_ref, me_ref, w_ref, own_ref, oth_ref, out_ref, g_ref, sems):
    first = pltpu.make_async_copy(own_ref, g_ref.at[0:HALF], sems.at[0])
    second = pltpu.make_async_copy(oth_ref, g_ref.at[HALF:SUBS], sems.at[1])
    first.start()
    second.start()
    first.wait()
    second.wait()
    core, y_me = me_ref[0], me_ref[1]

    def held(place):
        group = lax.shift_right_logical(place, 3)
        apart = lax.bitwise_and(y_me - lax.shift_right_logical(group, 1), 3)
        return lax.bitwise_xor(lax.bitwise_and(group, 1), core) * HALF + apart * 8 + lax.bitwise_and(place, 7)

    mine = held(me_ref[2])
    theirs = held(me_ref[4])
    out_ref[:, 0:M] = w_ref[0] * (g_ref[mine][:, 0:M] - g_ref[theirs][:, 0:M])
    lane = lanes((NRHS, 128))
    sums = [jnp.zeros((NRHS, 128), F32) for _ in range(NP // BLK)]
    scalars = jnp.zeros((NRHS, 128), F32)
    norm = jnp.zeros((NRHS, M), F32)
    for p in range(SUBS):
        mate = mate_ref[p]
        used = (mate >= 0).astype(F32)
        here = held(jnp.int32(p))
        at = held(jnp.maximum(mate, 0))
        tile = g_ref[here, :, M:W_U]
        scalars = scalars + tile
        limit = jnp.where(mate >= 0, cnt_ref[p], 0)
        piece = jnp.where(lane < limit, tile - g_ref[at, :, M:W_U], 0.0)
        if p % 16:
            piece = pltpu.roll(piece, 8 * (p % 16), 1)
        sums[p // 16] = sums[p // 16] + piece
        gone = g_ref[here, :, 0:M] - g_ref[at, :, 0:M]
        norm = norm + used * (gone * gone)
    for b in range(NP // BLK):
        out_ref[:, M + b * BLK:M + (b + 1) * BLK] = sums[b]
    scalars = jnp.where(lane == LANE_FF, 0.5 * jnp.sum(norm, axis=1, keepdims=True), scalars)
    out_ref[:, M + NP:W_X] = scalars


def choose_kernel(mate_ref, me_ref, z_ref, out_ref):
    lane = lanes((NRHS, 128))
    tail = jnp.where(lane < 8, z_ref[0, :, M:W_U], 0.0)
    for z in range(1, 8):
        tail = tail + pltpu.roll(jnp.where(lane < 8, z_ref[z, :, M:W_U], 0.0), 8 * z, 1)
    for group in range(8):
        mate = jnp.maximum(mate_ref[group * 8 + lax.bitwise_and(me_ref[2], 7)], 0)
        out_ref[group, :, 0:M] = z_ref[lax.bitwise_and(mate, 7), :, 0:M]
        out_ref[group, :, M:W_U] = tail


def match_kernel(mate_ref, cnt_ref, me_ref, w_ref, own_ref, got_ref, img_ref, sum_ref, q_ref):
    theirs = lax.shift_right_logical(me_ref[4], 3)
    img_ref[...] = w_ref[0] * (own_ref[0, :, 0:M] - got_ref[theirs][:, 0:M])
    lane = lanes((NRHS, 128))
    scalars = jnp.zeros((NRHS, 128), F32)
    for b in range(NP // BLK):
        both = got_ref[2 * b, :, M:W_U] + pltpu.roll(got_ref[2 * b + 1, :, M:W_U], 64, 1)
        q_ref[b] = both
        scalars = scalars + both
    for step in (8, 16, 32, 64):
        scalars = scalars + pltpu.roll(scalars, step, 1)
    for b in range(NP // BLK):
        total = jnp.zeros((NRHS, 128), F32)
        here = q_ref[b]
        for i in range(16):
            p = b * 16 + i
            mate = mate_ref[p]
            at = jnp.maximum(mate, 0)
            step = lax.bitwise_and(8 * (i - at), 127)
            there = pltpu.roll(q_ref[lax.shift_right_logical(at, 4)], step, 1)
            limit = 8 * i + jnp.where(mate >= 0, cnt_ref[p], 0)
            total = jnp.where((lane >= 8 * i) & (lane < limit), here - there, total)
        sum_ref[:, b * BLK:(b + 1) * BLK] = total
    sum_ref[:, NP:NP + 128] = scalars


def y_at(y_ref, place):
    tile = y_ref[lax.div(place, 16)]
    return pltpu.roll(tile, lax.rem(128 - 8 * lax.rem(place, 16), 128), 1)


def expand(y_ref, me_ref, w_ref, modes_ref, k):
    coeff = y_at(y_ref, me_ref[2]) - y_at(y_ref, me_ref[4 + k])
    total = coeff[:, 0:1] * modes_ref[k, 0:1, :]
    for m in range(1, MODES):
        total = total + coeff[:, m:m + 1] * modes_ref[k, m:m + 1, :]
    return w_ref[k] * total


def apply_panel(me_ref, w_ref, modes_ref, vectors, panel_ref, pay_ref, square):
    total = None
    for k in range(4):
        load = (w_ref[k] * vectors[k]).astype(BF16)
        at = pl.multiple_of(lax.bitwise_and(me_ref[3] - k, 3) * M, M)
        slot = panel_ref[0, :, pl.ds(at, M)]
        part = lax.dot_general(load, slot, (((1,), (1,)), ((), ())), preferred_element_type=F32)
        total = part if total is None else total + part
    lane = lanes((NRHS, 128))
    tail = jnp.zeros((NRHS, 128), F32)
    for m in range(MODES):
        tail = jnp.where(lane == m, jnp.sum(total * modes_ref[0, m:m + 1, :], axis=1, keepdims=True), tail)
    dots = jnp.sum(w_ref[0] * vectors[0] * total, axis=1, keepdims=True)
    tail = jnp.where(lane == LANE_DU, dots, tail)
    if square is not None:
        tail = jnp.where(lane == LANE_ZZ, 0.5 * jnp.sum(square * square, axis=1, keepdims=True), tail)
    for z in range(8):
        pay_ref[z, :, 0:M] = total
        pay_ref[z, :, M:W_U] = tail


def gathered_sums(x_refs, inv_ref, at=M):
    ms = x_refs[0][:, at:at + NP]
    scalars = x_refs[0][:, at + NP:at + NP + 128]
    for ref in x_refs[1:]:
        ms = ms + ref[:, at:at + NP]
        scalars = scalars + ref[:, at + NP:at + NP + 128]
    return ms, dot_pieces(ms, inv_ref), scalars


def first_kernel(me_ref, w_ref, x0, x1, x2, x3, inv_ref, yg_ref, gap_ref, modes_ref, panel_ref,
                 r_ref, z_ref, y_ref, pay_ref):
    xs = (x0, x1, x2, x3)
    _, solved, _ = gathered_sums(xs, inv_ref)
    for b in range(NP // BLK):
        y_ref[b] = yg_ref[b] - solved[:, b * BLK:(b + 1) * BLK]
    vectors = []
    for k in range(4):
        resid = w_ref[k] * w_ref[k] * gap_ref[k] - xs[k][:, 0:M]
        r_ref[k] = resid
        z = resid - expand(y_ref, me_ref, w_ref, modes_ref, k)
        z_ref[k] = z
        vectors.append(z)
    apply_panel(me_ref, w_ref, modes_ref, vectors, panel_ref, pay_ref, vectors[0])


def second_kernel(me_ref, w_ref, x0, x1, x2, x3, inv_ref, y_ref, r_ref, d_ref, lam_ref, modes_ref, panel_ref,
                  r_out, d_out, y_out, lam_out, rho_out, pay_ref):
    xs = (x0, x1, x2, x3)
    ms, solved, scalars = gathered_sums(xs, inv_ref)
    rho = scalars[:, LANE_ZZ:LANE_ZZ + 1]
    alpha = rho / scalars[:, LANE_DU:LANE_DU + 1]
    squared = scalars[:, LANE_FF:LANE_FF + 1] - jnp.sum(ms * solved, axis=1, keepdims=True)
    rho_new = jnp.maximum(alpha * alpha * squared - rho, 0.0)
    beta = rho_new / rho
    for b in range(NP // BLK):
        y_out[b] = y_ref[b] - alpha * solved[:, b * BLK:(b + 1) * BLK]
    vectors = []
    for k in range(4):
        resid = r_ref[k] - alpha * xs[k][:, 0:M]
        direction = resid - expand(y_out, me_ref, w_ref, modes_ref, k) + beta * d_ref[k]
        vectors.append(direction)
        if k == 0:
            r_out[...] = resid
            d_out[...] = direction
    lam_out[...] = lam_ref[...] + alpha * d_ref[0]
    rho_out[...] = jnp.broadcast_to(rho_new, (NRHS, 128))
    apply_panel(me_ref, w_ref, modes_ref, vectors, panel_ref, pay_ref, None)


def last_kernel(me_ref, w_ref, img_ref, x0, x1, x2, x3, inv_ref, y_ref, r_ref, d_ref, lam_ref, rho_ref, modes_ref,
                lam_out, z_out, y_out):
    xs = (x0, x1, x2, x3)
    _, solved, scalars = gathered_sums(xs, inv_ref, 0)
    alpha = rho_ref[:, 0:1] / scalars[:, LANE_DU:LANE_DU + 1]
    for b in range(NP // BLK):
        y_out[b] = y_ref[b] - alpha * solved[:, b * BLK:(b + 1) * BLK]
    resid = r_ref[...] - alpha * img_ref[...]
    lam_out[...] = lam_ref[...] + alpha * d_ref[...]
    z_out[...] = resid - expand(y_out, me_ref, w_ref, modes_ref, 0)


def prepare_kernel(own_ref, partner_ref, count_ref, modes_ref, gap_ref, loads_ref, out_ref, side_ref, tile_ref):
    own = own_ref[0]
    partner = partner_ref[0, 0]
    count = count_ref[own]
    weight = jnp.where(partner >= 0, jnp.where(own < partner, 1.0, -1.0), 0.0).astype(F32)
    out_ref[0:MODES, 0:M] = modes_ref[0, 0]
    out_ref[MODES:PAD, 0:M] = jnp.zeros((PAD - MODES, M), F32)
    out_ref[:, M:2 * M] = gap_ref[0, 0]
    side_ref[...] = jnp.zeros((128, M), F32)
    side_ref[0:8, :] = out_ref[:, 0:M]
    side_ref[16:24, :] = out_ref[:, M:2 * M]
    tile_ref[...] = jnp.zeros((PAD, 128), F32)
    tile_ref[0:MODES, 8:16] = loads_ref[0]
    products = lax.dot_general(
        out_ref[:, 0:M], side_ref[...], (((1,), (1,)), ((), ())), precision=HIGHEST, preferred_element_type=F32
    )
    lane = lanes((PAD, 128))
    active = rows_of((PAD, 128)) < count
    tile = jnp.where(lane < 8, products, jnp.where(active, tile_ref[...] + weight * products, 0.0))
    tile = jnp.where(lane == 6, partner.astype(F32), tile)
    out_ref[:, 2 * M:] = jnp.where(lane == 7, count.astype(F32), tile)


def shift(value, axis, step):
    size = lax.axis_size(axis)
    return lax.ppermute(value, axis, [(i, (i + step) % size) for i in range(size)])


def front_gather(value):
    return [value] + [shift(value, "x", k) for k in range(1, 4)]


def to_line(copies):
    return lax.all_to_all(copies, "z", 0, 0, tiled=True)


def sub_gather(copies):
    width = copies.shape[-1]
    along_z = to_line(copies)
    own = jnp.concatenate([along_z] + [shift(along_z, "y", k) for k in range(1, 4)], axis=0)
    other = shift(own, "c", 1)
    return own.reshape(HALF, NRHS, width), other.reshape(HALF, NRHS, width)


def sds(*shape):
    return jax.ShapeDtypeStruct(shape, F32)


def coarse_call(sub_counts, me, weights, near, far, modes_all, panels):
    return pl.pallas_call(
        coarse_kernel,
        out_shape=(
            jax.ShapeDtypeStruct((3, NP, NP), BF16), sds(4, NRHS, 128), sds(NRHS, M), sds(8, NRHS, W_U)
        ),
        in_specs=[SMEM, SMEM, SMEM, VMEM, VMEM, VMEM, ANY],
        out_specs=(VMEM,) * 4,
        scratch_shapes=[
            pltpu.VMEM((SUBS, PAD, 128), F32),
            pltpu.VMEM((NP, NP), F32),
            pltpu.VMEM((BLK, BLK), F32),
            pltpu.VMEM((4, NRHS, 128), F32),
            pltpu.VMEM((1, M, 4 * M), BF16),
            pltpu.SemaphoreType.DMA,
        ],
        compiler_params=pltpu.CompilerParams(vmem_limit_bytes=50 * 1024 * 1024),
        name="coarse",
    )(sub_counts, me, weights, near, far, modes_all, panels)


def shards(panels, gap, modes, mode_loads, partners, counts):
    z_me, y_me, c_me, x_me = (lax.axis_index(a) for a in ("z", "y", "c", "x"))
    own = (z_me * 4 + y_me) * 2 + c_me
    prepared = pl.pallas_call(
        prepare_kernel,
        out_shape=sds(PAD, 2 * M + 128),
        in_specs=[SMEM, SMEM, SMEM, VMEM, VMEM, VMEM],
        out_specs=VMEM,
        scratch_shapes=[pltpu.VMEM((128, M), F32), pltpu.VMEM((PAD, 128), F32)],
        compiler_params=PARAMS,
        name="prepare",
    )(own[None].astype(jnp.int32), partners, counts, modes, gap, mode_loads)
    gathered = front_gather(prepared)
    modes_all = jnp.stack([g[:, 0:M] for g in gathered])
    gap_all = jnp.stack([g[:, M:2 * M] for g in gathered])
    tiles = [g[:, 2 * M:] for g in gathered]
    packed = jnp.concatenate(
        [t[:, 0:8] for t in tiles]
        + [tiles[0][:, 8:16], tiles[0][:, 16:24] + tiles[1][:, 16:24] + tiles[2][:, 16:24] + tiles[3][:, 16:24]]
        + [jnp.zeros((PAD, 80), F32)],
        axis=1,
    )
    mates = jnp.stack([t[0, 6] for t in tiles]).astype(jnp.int32)
    weights = jnp.where(own < mates, 1.0, -1.0).astype(F32) * (mates >= 0).astype(F32)

    def place_of(sub):
        return jnp.where(sub >= 0, (sub & 7) * 8 + (sub >> 3), -1)

    me = jnp.concatenate(
        [jnp.stack([c_me, y_me, place_of(own), x_me]), jnp.maximum(place_of(mates), 0)]
    ).astype(jnp.int32)
    spread = jnp.broadcast_to(packed[None], (HALF, PAD, 128))
    near = lax.all_to_all(spread, ("z", "y"), 0, 0, tiled=True)
    far = shift(near, "c", 1)
    heads = jnp.stack([near[:, 0, 6], far[:, 0, 6]])
    heads = jnp.where(c_me == 0, heads, heads[::-1]).astype(jnp.int32).reshape(2, 8, 4)
    mate_places = place_of(heads.transpose(2, 0, 1).reshape(SUBS))
    sub_counts = counts.reshape(8, 8).T.reshape(SUBS)
    near, far, mate_places = lax.optimization_barrier((near, far, mate_places))

    inverse, y_gap, lam, payload = coarse_call(
        sub_counts, me, weights, near, far, modes_all, panels
    )

    def exchange_all(payload):
        return pl.pallas_call(
            mate_kernel,
            out_shape=sds(NRHS, W_X),
            in_specs=[SMEM] * 4 + [ANY, ANY],
            out_specs=VMEM,
            scratch_shapes=[pltpu.VMEM((SUBS, NRHS, W_U), F32), pltpu.SemaphoreType.DMA((2,))],
            compiler_params=PARAMS,
            name="mate",
        )(mate_places, sub_counts, me, weights, *sub_gather(payload))

    def exchange(payload, name):
        chosen = pl.pallas_call(
            choose_kernel,
            out_shape=sds(8, NRHS, W_U),
            in_specs=[SMEM, SMEM, VMEM],
            out_specs=VMEM,
            compiler_params=PARAMS,
            name="choose_" + name,
        )(mate_places, me, to_line(payload))
        got = lax.all_to_all(chosen, ("y", "c"), 0, 0, tiled=True)
        return pl.pallas_call(
            match_kernel,
            out_shape=(sds(NRHS, M), sds(NRHS, NP + 128)),
            in_specs=[SMEM] * 4 + [VMEM, VMEM],
            out_specs=(VMEM, VMEM),
            scratch_shapes=[pltpu.VMEM((4, NRHS, 128), F32)],
            compiler_params=PARAMS,
            name="match_" + name,
        )(mate_places, sub_counts, me, weights, payload, got)

    xs = front_gather(jnp.concatenate(exchange(payload, "begin"), axis=1))
    resid, direction, y_resid, payload = pl.pallas_call(
        first_kernel,
        out_shape=(sds(4, NRHS, M), sds(4, NRHS, M), sds(4, NRHS, 128), sds(8, NRHS, W_U)),
        in_specs=[SMEM, SMEM] + [VMEM] * 9,
        out_specs=(VMEM,) * 4,
        compiler_params=PARAMS,
        name="first",
    )(me, weights, *xs, inverse, y_gap, gap_all, modes_all, panels)

    xs = front_gather(exchange_all(payload))
    resid, direction, y_resid, lam, rho, payload = pl.pallas_call(
        second_kernel,
        out_shape=(sds(NRHS, M), sds(NRHS, M), sds(4, NRHS, 128), sds(NRHS, M), sds(NRHS, 128), sds(8, NRHS, W_U)),
        in_specs=[SMEM, SMEM] + [VMEM] * 11,
        out_specs=(VMEM,) * 6,
        compiler_params=PARAMS,
        name="second",
    )(me, weights, *xs, inverse, y_resid, resid, direction, lam, modes_all, panels)

    image, sums = exchange(payload, "second")
    xs = front_gather(sums)
    lam, projected, _ = pl.pallas_call(
        last_kernel,
        out_shape=(sds(NRHS, M), sds(NRHS, M), sds(4, NRHS, 128)),
        in_specs=[SMEM, SMEM] + [VMEM] * 12,
        out_specs=(VMEM,) * 3,
        compiler_params=PARAMS,
        name="last",
    )(me, weights, image, *xs, inverse, y_resid, resid, direction, lam, rho, modes_all)
    return (lam[None, None], projected[None, None])


def solution(mesh):
    fine = Mesh(mesh.devices.reshape(8, 4, 2, 4), ("z", "y", "c", "x"))
    sub = ("z", "y", "c")
    in_specs = (
        P(sub, "x", None),
        P(sub, "x", None, None),
        P(sub, "x", None, None),
        P(sub, None, None),
        P(sub, "x"),
        P(),
    )
    out_specs = (P(sub, "x", None, None), P(sub, "x", None, None))
    return jax.shard_map(shards, mesh=fine, in_specs=in_specs, out_specs=out_specs, check_vma=False)
```

```python
import functools

import jax
import jax.numpy as jnp
from jax import lax
from jax.experimental import pallas as pl
from jax.experimental.pallas import tpu as pltpu
from jax.sharding import Mesh, PartitionSpec as P

MODES = 6
NRHS = 8
M = 768
SUBS = 64
PAD = 8
NP = SUBS * PAD
BLK = 128
HALF = SUBS // 2
HIGHEST = lax.Precision.HIGHEST
F32 = jnp.float32
BF16 = jnp.bfloat16

LANE_DU, LANE_ZZ, LANE_FF = 6, 7, 8
W_U = M + 128
W_X = M + NP + 128

SMEM = pl.BlockSpec(memory_space=pltpu.SMEM)
VMEM = pl.BlockSpec(memory_space=pltpu.VMEM)
ANY = pl.BlockSpec(memory_space=pl.ANY)
PARAMS = pltpu.CompilerParams(vmem_limit_bytes=16 * 1024 * 1024)


def lanes(shape):
    return lax.broadcasted_iota(jnp.int32, shape, len(shape) - 1)


def rows_of(shape):
    return lax.broadcasted_iota(jnp.int32, shape, 0)


def dot_high(a, b):
    return jnp.dot(a, b, precision=HIGHEST, preferred_element_type=F32)


def split(x):
    high = x.astype(BF16).astype(F32)
    rest = x - high
    middle = rest.astype(BF16).astype(F32)
    return high, middle, rest - middle


def dot_six(a, b):
    ah, am, al = (p.astype(BF16) for p in split(a))
    bh, bm, bl = (p.astype(BF16) for p in split(b))
    left = jnp.concatenate([ah, am, ah, am, ah, al], axis=1)
    right = jnp.concatenate([bh, bh, bm, bm, bl, bh], axis=0)
    return jnp.dot(left, right, preferred_element_type=F32)


def dot_pieces(a, pieces_ref):
    stacked = jnp.concatenate(split(a), axis=0)
    rows = a.shape[0]
    part = jnp.dot(stacked.astype(BF16), pieces_ref[0], preferred_element_type=F32)
    total = part[0:rows] + part[rows:2 * rows] + part[2 * rows:3 * rows]
    part = jnp.dot(stacked[0:2 * rows].astype(BF16), pieces_ref[1], preferred_element_type=F32)
    total = total + (part[0:rows] + part[rows:2 * rows])
    return total + jnp.dot(stacked[0:rows].astype(BF16), pieces_ref[2], preferred_element_type=F32)


def coarse_kernel(cnt_ref, me_ref, w_ref, own_ref, oth_ref, modes_ref, panel_ref,
                  inv_ref, yg_ref, lam_ref, pay_ref, g_ref, a_ref, d_ref, y0_ref, held_ref, sem):
    copy = pltpu.make_async_copy(panel_ref, held_ref, sem)
    copy.start()
    core = me_ref[0]
    for y in range(4):
        for z in range(8):
            g_ref[2 * y * 8 + core * 8 + z] = own_ref[z * 4 + y]
            g_ref[2 * y * 8 + (1 - core) * 8 + z] = oth_ref[z * 4 + y]
    flipped = g_ref[...].reshape(NP, 128).T
    column = lanes((PAD, NP))
    row = rows_of((PAD, NP))
    column_sub = lax.shift_right_logical(column, 3)
    column_active = lax.bitwise_and(column, 7) < flipped[7:8, :].astype(jnp.int32)
    grams, places = [], []
    for k in range(4):
        mate = jnp.broadcast_to(flipped[8 * k + 6:8 * k + 7, :].astype(jnp.int32), (PAD, NP))
        places.append(lax.bitwise_and(mate, 7) * 8 + lax.shift_right_logical(mate, 3))
        keep = (row < MODES) & column_active & (mate >= 0)
        grams.append(jnp.where(keep, flipped[8 * k:8 * k + 8, :], 0.0))
    whole = grams[0] + grams[1] + grams[2] + grams[3]
    for t in range(SUBS):
        total = jnp.where(column_sub == t, whole, 0.0)
        for k in range(4):
            total = total - jnp.where(places[k] == t, grams[k], 0.0)
        identity = jnp.where(column == PAD * t + row, 1.0, 0.0)
        a_ref[PAD * t:PAD * t + PAD, :] = jnp.where(row < cnt_ref[t], total, identity)
    lane = lanes((BLK, BLK))

    tile_lane = lanes((PAD, BLK))
    tile_row = rows_of((PAD, BLK))

    def sweep(i, pivots):
        p = PAD * i
        rows = d_ref[p:p + PAD, :]
        columns = [jnp.broadcast_to(rows[:, p + b:p + b + 1], (PAD, BLK)) for b in range(pivots)]
        s = [[None] * pivots for _ in range(pivots)]
        for b in range(pivots):
            for a in range(b + 1):
                s[a][b] = jnp.broadcast_to(columns[b][a:a + 1, :], (PAD, BLK))
        for v in range(pivots):
            over = 1.0 / s[v][v]
            line = [s[min(v, b)][max(v, b)] for b in range(pivots)]
            scaled = [x * over for x in line]
            for a in range(pivots):
                for b in range(a, pivots):
                    if a != v and b != v:
                        s[a][b] = s[a][b] - line[a] * scaled[b]
            for b in range(pivots):
                if b != v:
                    s[min(v, b)][max(v, b)] = scaled[b]
            s[v][v] = -over
        new_rows = jnp.zeros((PAD, BLK), F32)
        tails = []
        for b in range(pivots):
            column = jnp.zeros((PAD, BLK), F32)
            for a in range(pivots):
                column = jnp.where(tile_row == a, s[min(a, b)][max(a, b)], column)
            new_rows = new_rows - column * rows[b:b + 1, :]
            tails.append(column)
        for b in range(pivots):
            new_rows = jnp.where(tile_lane == p + b, tails[b], new_rows)
        mat = d_ref[...]
        new = jnp.where((lane >= p) & (lane < p + pivots), 0.0, mat)
        for b in range(pivots):
            new = new - mat[:, p + b:p + b + 1] * new_rows[b:b + 1, :]
        d_ref[...] = new
        d_ref[p:p + PAD, :] = jnp.where(tile_row < pivots, new_rows, rows)

    for b in range(NP // BLK):
        lo, hi = b * BLK, (b + 1) * BLK
        d_ref[...] = a_ref[lo:hi, lo:hi]

        for i in range(BLK // PAD):
            count = cnt_ref[b * (BLK // PAD) + i]
            for low, high in ((1, 3), (4, 6)):
                @pl.when((count >= low) & (count <= high))
                def _(i=i, high=high):
                    sweep(i, high)

        small = -d_ref[...]
        tall = a_ref[:, lo:hi]
        wide = dot_six(small, a_ref[lo:hi, :])
        both = dot_six(tall, jnp.concatenate([wide, small], axis=1))
        a_ref[...] = a_ref[...] - both[:, 0:NP]
        a_ref[:, lo:hi] = both[:, NP:]
        a_ref[lo:hi, :] = wide
        a_ref[lo:hi, lo:hi] = -small
    pieces = split(-a_ref[...])
    for n in range(3):
        inv_ref[n] = pieces[n].astype(BF16)
    y = dot_pieces(flipped[32:48, :], inv_ref)
    for b in range(NP // BLK):
        y0_ref[b] = y[0:8, b * BLK:(b + 1) * BLK]
        yg_ref[b] = y[8:16, b * BLK:(b + 1) * BLK]
    vectors = [expand(y0_ref, me_ref, w_ref, modes_ref, k) for k in range(4)]
    lam_ref[...] = vectors[0]
    copy.wait()
    apply_panel(me_ref, w_ref, modes_ref, vectors, held_ref, pay_ref, None)


def mate_kernel(mate_ref, cnt_ref, me_ref, w_ref, own_ref, oth_ref, out_ref, g_ref, sems):
    first = pltpu.make_async_copy(own_ref, g_ref.at[0:HALF], sems.at[0])
    second = pltpu.make_async_copy(oth_ref, g_ref.at[HALF:SUBS], sems.at[1])
    first.start()
    second.start()
    first.wait()
    second.wait()
    core, y_me = me_ref[0], me_ref[1]

    def held(place):
        group = lax.shift_right_logical(place, 3)
        apart = lax.bitwise_and(y_me - lax.shift_right_logical(group, 1), 3)
        return lax.bitwise_xor(lax.bitwise_and(group, 1), core) * HALF + apart * 8 + lax.bitwise_and(place, 7)

    mine = held(me_ref[2])
    theirs = held(me_ref[4])
    out_ref[:, 0:M] = w_ref[0] * (g_ref[mine][:, 0:M] - g_ref[theirs][:, 0:M])
    lane = lanes((NRHS, 128))
    sums = [jnp.zeros((NRHS, 128), F32) for _ in range(NP // BLK)]
    scalars = jnp.zeros((NRHS, 128), F32)
    norm = jnp.zeros((NRHS, M), F32)
    for p in range(SUBS):
        mate = mate_ref[p]
        used = (mate >= 0).astype(F32)
        here = held(jnp.int32(p))
        at = held(jnp.maximum(mate, 0))
        tile = g_ref[here, :, M:W_U]
        scalars = scalars + tile
        limit = jnp.where(mate >= 0, cnt_ref[p], 0)
        piece = jnp.where(lane < limit, tile - g_ref[at, :, M:W_U], 0.0)
        if p % 16:
            piece = pltpu.roll(piece, 8 * (p % 16), 1)
        sums[p // 16] = sums[p // 16] + piece
        gone = g_ref[here, :, 0:M] - g_ref[at, :, 0:M]
        norm = norm + used * (gone * gone)
    for b in range(NP // BLK):
        out_ref[:, M + b * BLK:M + (b + 1) * BLK] = sums[b]
    scalars = jnp.where(lane == LANE_FF, 0.5 * jnp.sum(norm, axis=1, keepdims=True), scalars)
    out_ref[:, M + NP:W_X] = scalars


def choose_kernel(mate_ref, me_ref, z_ref, out_ref):
    lane = lanes((NRHS, 128))
    tail = jnp.where(lane < 8, z_ref[0, :, M:W_U], 0.0)
    for z in range(1, 8):
        tail = tail + pltpu.roll(jnp.where(lane < 8, z_ref[z, :, M:W_U], 0.0), 8 * z, 1)
    for group in range(8):
        mate = jnp.maximum(mate_ref[group * 8 + lax.bitwise_and(me_ref[2], 7)], 0)
        out_ref[group, :, 0:M] = z_ref[lax.bitwise_and(mate, 7), :, 0:M]
        out_ref[group, :, M:W_U] = tail


def match_kernel(mate_ref, cnt_ref, me_ref, w_ref, own_ref, got_ref, img_ref, sum_ref, q_ref):
    theirs = lax.shift_right_logical(me_ref[4], 3)
    img_ref[...] = w_ref[0] * (own_ref[0, :, 0:M] - got_ref[theirs][:, 0:M])
    lane = lanes((NRHS, 128))
    scalars = jnp.zeros((NRHS, 128), F32)
    for b in range(NP // BLK):
        both = got_ref[2 * b, :, M:W_U] + pltpu.roll(got_ref[2 * b + 1, :, M:W_U], 64, 1)
        q_ref[b] = both
        scalars = scalars + both
    for step in (8, 16, 32, 64):
        scalars = scalars + pltpu.roll(scalars, step, 1)
    for b in range(NP // BLK):
        total = jnp.zeros((NRHS, 128), F32)
        here = q_ref[b]
        for i in range(16):
            p = b * 16 + i
            mate = mate_ref[p]
            at = jnp.maximum(mate, 0)
            step = lax.bitwise_and(8 * (i - at), 127)
            there = pltpu.roll(q_ref[lax.shift_right_logical(at, 4)], step, 1)
            limit = 8 * i + jnp.where(mate >= 0, cnt_ref[p], 0)
            total = jnp.where((lane >= 8 * i) & (lane < limit), here - there, total)
        sum_ref[:, b * BLK:(b + 1) * BLK] = total
    sum_ref[:, NP:NP + 128] = scalars


def y_at(y_ref, place):
    tile = y_ref[lax.div(place, 16)]
    return pltpu.roll(tile, lax.rem(128 - 8 * lax.rem(place, 16), 128), 1)


def expand(y_ref, me_ref, w_ref, modes_ref, k):
    coeff = y_at(y_ref, me_ref[2]) - y_at(y_ref, me_ref[4 + k])
    total = coeff[:, 0:1] * modes_ref[k, 0:1, :]
    for m in range(1, MODES):
        total = total + coeff[:, m:m + 1] * modes_ref[k, m:m + 1, :]
    return w_ref[k] * total


def apply_panel(me_ref, w_ref, modes_ref, vectors, panel_ref, pay_ref, square):
    total = None
    for k in range(4):
        load = (w_ref[k] * vectors[k]).astype(BF16)
        at = pl.multiple_of(lax.bitwise_and(me_ref[3] - k, 3) * M, M)
        slot = panel_ref[0, :, pl.ds(at, M)]
        part = lax.dot_general(load, slot, (((1,), (1,)), ((), ())), preferred_element_type=F32)
        total = part if total is None else total + part
    lane = lanes((NRHS, 128))
    tail = jnp.zeros((NRHS, 128), F32)
    for m in range(MODES):
        tail = jnp.where(lane == m, jnp.sum(total * modes_ref[0, m:m + 1, :], axis=1, keepdims=True), tail)
    dots = jnp.sum(w_ref[0] * vectors[0] * total, axis=1, keepdims=True)
    tail = jnp.where(lane == LANE_DU, dots, tail)
    if square is not None:
        tail = jnp.where(lane == LANE_ZZ, 0.5 * jnp.sum(square * square, axis=1, keepdims=True), tail)
    for z in range(8):
        pay_ref[z, :, 0:M] = total
        pay_ref[z, :, M:W_U] = tail


def gathered_sums(x_refs, inv_ref, at=M):
    ms = x_refs[0][:, at:at + NP]
    scalars = x_refs[0][:, at + NP:at + NP + 128]
    for ref in x_refs[1:]:
        ms = ms + ref[:, at:at + NP]
        scalars = scalars + ref[:, at + NP:at + NP + 128]
    return ms, dot_pieces(ms, inv_ref), scalars


def first_kernel(me_ref, w_ref, x0, x1, x2, x3, inv_ref, yg_ref, gap_ref, modes_ref, panel_ref,
                 r_ref, z_ref, y_ref, pay_ref):
    xs = (x0, x1, x2, x3)
    _, solved, _ = gathered_sums(xs, inv_ref)
    for b in range(NP // BLK):
        y_ref[b] = yg_ref[b] - solved[:, b * BLK:(b + 1) * BLK]
    vectors = []
    for k in range(4):
        resid = w_ref[k] * w_ref[k] * gap_ref[k] - xs[k][:, 0:M]
        r_ref[k] = resid
        z = resid - expand(y_ref, me_ref, w_ref, modes_ref, k)
        z_ref[k] = z
        vectors.append(z)
    apply_panel(me_ref, w_ref, modes_ref, vectors, panel_ref, pay_ref, vectors[0])


def second_kernel(me_ref, w_ref, x0, x1, x2, x3, inv_ref, y_ref, r_ref, d_ref, lam_ref, modes_ref, panel_ref,
                  r_out, d_out, y_out, lam_out, rho_out, pay_ref):
    xs = (x0, x1, x2, x3)
    ms, solved, scalars = gathered_sums(xs, inv_ref)
    rho = scalars[:, LANE_ZZ:LANE_ZZ + 1]
    alpha = rho / scalars[:, LANE_DU:LANE_DU + 1]
    squared = scalars[:, LANE_FF:LANE_FF + 1] - jnp.sum(ms * solved, axis=1, keepdims=True)
    rho_new = jnp.maximum(alpha * alpha * squared - rho, 0.0)
    beta = rho_new / rho
    for b in range(NP // BLK):
        y_out[b] = y_ref[b] - alpha * solved[:, b * BLK:(b + 1) * BLK]
    vectors = []
    for k in range(4):
        resid = r_ref[k] - alpha * xs[k][:, 0:M]
        direction = resid - expand(y_out, me_ref, w_ref, modes_ref, k) + beta * d_ref[k]
        vectors.append(direction)
        if k == 0:
            r_out[...] = resid
            d_out[...] = direction
    lam_out[...] = lam_ref[...] + alpha * d_ref[0]
    rho_out[...] = jnp.broadcast_to(rho_new, (NRHS, 128))
    apply_panel(me_ref, w_ref, modes_ref, vectors, panel_ref, pay_ref, None)


def last_kernel(me_ref, w_ref, img_ref, x0, x1, x2, x3, inv_ref, y_ref, r_ref, d_ref, lam_ref, rho_ref, modes_ref,
                lam_out, z_out, y_out):
    xs = (x0, x1, x2, x3)
    _, solved, scalars = gathered_sums(xs, inv_ref, 0)
    alpha = rho_ref[:, 0:1] / scalars[:, LANE_DU:LANE_DU + 1]
    for b in range(NP // BLK):
        y_out[b] = y_ref[b] - alpha * solved[:, b * BLK:(b + 1) * BLK]
    resid = r_ref[...] - alpha * img_ref[...]
    lam_out[...] = lam_ref[...] + alpha * d_ref[...]
    z_out[...] = resid - expand(y_out, me_ref, w_ref, modes_ref, 0)


def prepare_kernel(own_ref, partner_ref, count_ref, modes_ref, gap_ref, loads_ref, out_ref, side_ref, tile_ref):
    own = own_ref[0]
    partner = partner_ref[0, 0]
    count = count_ref[own]
    weight = jnp.where(partner >= 0, jnp.where(own < partner, 1.0, -1.0), 0.0).astype(F32)
    out_ref[0:MODES, 0:M] = modes_ref[0, 0]
    out_ref[MODES:PAD, 0:M] = jnp.zeros((PAD - MODES, M), F32)
    out_ref[:, M:2 * M] = gap_ref[0, 0]
    side_ref[...] = jnp.zeros((128, M), F32)
    side_ref[0:8, :] = out_ref[:, 0:M]
    side_ref[16:24, :] = out_ref[:, M:2 * M]
    tile_ref[...] = jnp.zeros((PAD, 128), F32)
    tile_ref[0:MODES, 8:16] = loads_ref[0]
    products = lax.dot_general(
        out_ref[:, 0:M], side_ref[...], (((1,), (1,)), ((), ())), precision=HIGHEST, preferred_element_type=F32
    )
    lane = lanes((PAD, 128))
    active = rows_of((PAD, 128)) < count
    tile = jnp.where(lane < 8, products, jnp.where(active, tile_ref[...] + weight * products, 0.0))
    tile = jnp.where(lane == 6, partner.astype(F32), tile)
    out_ref[:, 2 * M:] = jnp.where(lane == 7, count.astype(F32), tile)


def shift(value, axis, step):
    size = lax.axis_size(axis)
    return lax.ppermute(value, axis, [(i, (i + step) % size) for i in range(size)])


def front_gather(value):
    return [value] + [shift(value, "x", k) for k in range(1, 4)]


def to_line(copies):
    return lax.all_to_all(copies, "z", 0, 0, tiled=True)


def sub_gather(copies):
    width = copies.shape[-1]
    along_z = to_line(copies)
    own = jnp.concatenate([along_z] + [shift(along_z, "y", k) for k in range(1, 4)], axis=0)
    other = shift(own, "c", 1)
    return own.reshape(HALF, NRHS, width), other.reshape(HALF, NRHS, width)


def sds(*shape):
    return jax.ShapeDtypeStruct(shape, F32)


def coarse_call(sub_counts, me, weights, near, far, modes_all, panels):
    return pl.pallas_call(
        coarse_kernel,
        out_shape=(
            jax.ShapeDtypeStruct((3, NP, NP), BF16), sds(4, NRHS, 128), sds(NRHS, M), sds(8, NRHS, W_U)
        ),
        in_specs=[SMEM, SMEM, SMEM, VMEM, VMEM, VMEM, ANY],
        out_specs=(VMEM,) * 4,
        scratch_shapes=[
            pltpu.VMEM((SUBS, PAD, 128), F32),
            pltpu.VMEM((NP, NP), F32),
            pltpu.VMEM((BLK, BLK), F32),
            pltpu.VMEM((4, NRHS, 128), F32),
            pltpu.VMEM((1, M, 4 * M), BF16),
            pltpu.SemaphoreType.DMA,
        ],
        compiler_params=pltpu.CompilerParams(vmem_limit_bytes=50 * 1024 * 1024),
        name="coarse",
    )(sub_counts, me, weights, near, far, modes_all, panels)


def shards(panels, gap, modes, mode_loads, partners, counts):
    z_me, y_me, c_me, x_me = (lax.axis_index(a) for a in ("z", "y", "c", "x"))
    own = (z_me * 4 + y_me) * 2 + c_me
    prepared = pl.pallas_call(
        prepare_kernel,
        out_shape=sds(PAD, 2 * M + 128),
        in_specs=[SMEM, SMEM, SMEM, VMEM, VMEM, VMEM],
        out_specs=VMEM,
        scratch_shapes=[pltpu.VMEM((128, M), F32), pltpu.VMEM((PAD, 128), F32)],
        compiler_params=PARAMS,
        name="prepare",
    )(own[None].astype(jnp.int32), partners, counts, modes, gap, mode_loads)
    gathered = front_gather(prepared)
    modes_all = jnp.stack([g[:, 0:M] for g in gathered])
    gap_all = jnp.stack([g[:, M:2 * M] for g in gathered])
    tiles = [g[:, 2 * M:] for g in gathered]
    packed = jnp.concatenate(
        [t[:, 0:8] for t in tiles]
        + [tiles[0][:, 8:16], tiles[0][:, 16:24] + tiles[1][:, 16:24] + tiles[2][:, 16:24] + tiles[3][:, 16:24]]
        + [jnp.zeros((PAD, 80), F32)],
        axis=1,
    )
    mates = jnp.stack([t[0, 6] for t in tiles]).astype(jnp.int32)
    weights = jnp.where(own < mates, 1.0, -1.0).astype(F32) * (mates >= 0).astype(F32)

    def place_of(sub):
        return jnp.where(sub >= 0, (sub & 7) * 8 + (sub >> 3), -1)

    me = jnp.concatenate(
        [jnp.stack([c_me, y_me, place_of(own), x_me]), jnp.maximum(place_of(mates), 0)]
    ).astype(jnp.int32)
    spread = jnp.broadcast_to(packed[None], (HALF, PAD, 128))
    near = lax.all_to_all(spread, ("z", "y"), 0, 0, tiled=True)
    far = shift(near, "c", 1)
    heads = jnp.stack([near[:, 0, 6], far[:, 0, 6]])
    heads = jnp.where(c_me == 0, heads, heads[::-1]).astype(jnp.int32).reshape(2, 8, 4)
    mate_places = place_of(heads.transpose(2, 0, 1).reshape(SUBS))
    sub_counts = counts.reshape(8, 8).T.reshape(SUBS)
    near, far, mate_places = lax.optimization_barrier((near, far, mate_places))

    inverse, y_gap, lam, payload = coarse_call(
        sub_counts, me, weights, near, far, modes_all, panels
    )

    def exchange_all(payload):
        return pl.pallas_call(
            mate_kernel,
            out_shape=sds(NRHS, W_X),
            in_specs=[SMEM] * 4 + [ANY, ANY],
            out_specs=VMEM,
            scratch_shapes=[pltpu.VMEM((SUBS, NRHS, W_U), F32), pltpu.SemaphoreType.DMA((2,))],
            compiler_params=PARAMS,
            name="mate",
        )(mate_places, sub_counts, me, weights, *sub_gather(payload))

    def exchange(payload, name):
        chosen = pl.pallas_call(
            choose_kernel,
            out_shape=sds(8, NRHS, W_U),
            in_specs=[SMEM, SMEM, VMEM],
            out_specs=VMEM,
            compiler_params=PARAMS,
            name="choose_" + name,
        )(mate_places, me, to_line(payload))
        got = lax.all_to_all(chosen, ("y", "c"), 0, 0, tiled=True)
        return pl.pallas_call(
            match_kernel,
            out_shape=(sds(NRHS, M), sds(NRHS, NP + 128)),
            in_specs=[SMEM] * 4 + [VMEM, VMEM],
            out_specs=(VMEM, VMEM),
            scratch_shapes=[pltpu.VMEM((4, NRHS, 128), F32)],
            compiler_params=PARAMS,
            name="match_" + name,
        )(mate_places, sub_counts, me, weights, payload, got)

    xs = front_gather(jnp.concatenate(exchange(payload, "begin"), axis=1))
    resid, direction, y_resid, payload = pl.pallas_call(
        first_kernel,
        out_shape=(sds(4, NRHS, M), sds(4, NRHS, M), sds(4, NRHS, 128), sds(8, NRHS, W_U)),
        in_specs=[SMEM, SMEM] + [VMEM] * 9,
        out_specs=(VMEM,) * 4,
        compiler_params=PARAMS,
        name="first",
    )(me, weights, *xs, inverse, y_gap, gap_all, modes_all, panels)

    xs = front_gather(exchange_all(payload))
    resid, direction, y_resid, lam, rho, payload = pl.pallas_call(
        second_kernel,
        out_shape=(sds(NRHS, M), sds(NRHS, M), sds(4, NRHS, 128), sds(NRHS, M), sds(NRHS, 128), sds(8, NRHS, W_U)),
        in_specs=[SMEM, SMEM] + [VMEM] * 11,
        out_specs=(VMEM,) * 6,
        compiler_params=PARAMS,
        name="second",
    )(me, weights, *xs, inverse, y_resid, resid, direction, lam, modes_all, panels)

    image, sums = exchange(payload, "second")
    xs = front_gather(sums)
    lam, projected, _ = pl.pallas_call(
        last_kernel,
        out_shape=(sds(NRHS, M), sds(NRHS, M), sds(4, NRHS, 128)),
        in_specs=[SMEM, SMEM] + [VMEM] * 12,
        out_specs=(VMEM,) * 3,
        compiler_params=PARAMS,
        name="last",
    )(me, weights, image, *xs, inverse, y_resid, resid, direction, lam, rho, modes_all)
    return (lam[None, None], projected[None, None])


def solution(mesh):
    fine = Mesh(mesh.devices.reshape(8, 4, 2, 4), ("z", "y", "c", "x"))
    sub = ("z", "y", "c")
    in_specs = (
        P(sub, "x", None),
        P(sub, "x", None, None),
        P(sub, "x", None, None),
        P(sub, None, None),
        P(sub, "x"),
        P(),
    )
    out_specs = (P(sub, "x", None, None), P(sub, "x", None, None))
    return jax.shard_map(shards, mesh=fine, in_specs=in_specs, out_specs=out_specs, check_vma=False)
```
